32 devices in a mesh: band: 16 (over z, x, core), var: 2 (over y).
Axes of the slice: x: 2, y: 2, z: 4, core: 2. Of those that a mesh axis runs over, the one named last changes fastest.
Arguments:
- pixels: bfloat16 [16, 16, 4096], P('var', None, 'band'), may hold values from -6 to 6
- embed_weight: bfloat16 [16, 16, 1024], P('var'), may hold values from -1.5 to 1.5
- variable_embed: bfloat16 [16, 1024], P('var'), may hold values from -6 to 6
- agg_key: bfloat16 [1024, 16], replicated, may hold values from -0.1875 to 0.1875
- agg_value: bfloat16 [1024, 1024], replicated, may hold values from -0.1875 to 0.1875
- position: bfloat16 [4096, 1024], P(('band', 'var')), may hold values from -6 to 6
- qkv_weight: bfloat16 [1024, 3, 1024], P(None, None, 'var'), may hold values from -0.375 to 0.375
- out_weight: bfloat16 [1024, 1024], P('var'), may hold values from -0.1875 to 0.1875
Outputs:
- block_out: bfloat16 [4096, 1024], P(('band', 'var'))
The draws below stay inside these ranges and needn't reach their ends.
All inputs are finite; a program needn't handle non-finite values.
Results may differ from the reference program's by a relative error of at most 0.015.
The reference program's roundings to bfloat16 on the way count: a program that leaves them out, or rounds other values in their place, can miss the bound.
Values may be sent and summed in bfloat16 or wider, within the bound.
No kernel may reach another device: no remote copies, remote signals or barrier semaphores. Data moves between devices by JAX's collectives and lax.ppermute only.
A program may use at most 64 MiB of HBM per device.

```python
import jax
import jax.numpy as jnp
from jax import lax

D = 1024
HEADS = 16
HEAD_DIM = 64
VARS = 16
PIX = 16
REACH = 1
BAND_TOK = 256
TOKENS = 4096
N_BAND = 16


def block_scale(own_key, dims, cuts, least, high):
    gain, own = 1.0, jax.random.fold_in(own_key, 6)
    for dim, shards_of in cuts:
        draws = jnp.exp(jax.random.uniform(jax.random.fold_in(own, dim), (shards_of,), jnp.float32, least / len(cuts), high / len(cuts)))
        gain = gain * jnp.repeat(draws, dims[dim] // shards_of).reshape([-1 if axis == dim else 1 for axis in range(len(dims))])
    return gain


def bell_draw(stream_key, shape, deviation, bound, pieces=(), held_as=jnp.bfloat16):
    values = jax.random.normal(stream_key, shape, jnp.float32) * deviation
    if len(pieces) > 0:
        values = block_scale(stream_key, shape, pieces, -0.22, 0.18) * values
    return jnp.clip(values, min=-bound, max=bound).astype(held_as)


def setup_inputs(seed: int = 0) -> dict:
    streams_of = jax.random.split(jax.random.key(seed), 9)
    pixels = bell_draw(streams_of[0], (VARS, PIX, TOKENS), 1.0, 6.0, ((0, 2), (2, 16)))
    embed_weight = bell_draw(streams_of[1], (VARS, PIX, D), PIX ** -0.5, 1.5, ((0, 2),))
    variable_embed = bell_draw(streams_of[2], (VARS, D), 1.0, 6.0, ((0, 2),))
    agg_key = bell_draw(streams_of[3], (D, HEADS), D ** -0.5, 0.1875)
    agg_value = bell_draw(streams_of[4], (D, D), D ** -0.5, 0.1875)
    position = bell_draw(streams_of[5], (TOKENS, D), 1.0, 6.0, ((0, 32),))
    qkv_weight = bell_draw(streams_of[6], (D, 3, D), (D // 4) ** -0.5, 0.375, ((2, 2),))
    out_weight = bell_draw(streams_of[7], (D, D), D ** -0.5, 0.1875, ((0, 2),))
    return {"pixels": pixels, "embed_weight": embed_weight, "variable_embed": variable_embed, "agg_key": agg_key, "agg_value": agg_value, "position": position, "qkv_weight": qkv_weight, "out_weight": out_weight}


epsilon = 1e-05

def embed_vars(pixel_rows, table, offsets):
    summed = jnp.einsum('vpt,vpd->vtd', pixel_rows.astype(jnp.float32), table.astype(jnp.float32))
    return (summed + offsets.astype(jnp.float32)[:, None, :]).astype(jnp.bfloat16)

def normalize(values):
    centre = lax.optimization_barrier(jnp.mean(values, axis=-1, keepdims=True))
    spread = lax.optimization_barrier(jnp.mean(jnp.square(values - centre), axis=-1, keepdims=True))
    return (values - centre) * lax.rsqrt(spread + epsilon)

def reference(pixels, embed_weight, variable_embed, agg_key, agg_value, position, qkv_weight, out_weight):
    value_heads = agg_value.astype(jnp.float32).reshape(D, HEADS, HEAD_DIM)

    def front(band_index):
        start_row = band_index * BAND_TOK
        pixel_rows = lax.dynamic_slice_in_dim(pixels, start_row, BAND_TOK, 2)
        embedded = embed_vars(pixel_rows, embed_weight, variable_embed)
        scores = jnp.einsum('vtd,dh->tvh', embedded.astype(jnp.float32), agg_key.astype(jnp.float32))
        expos = jnp.exp(scores)
        weights = (expos / lax.optimization_barrier(jnp.sum(expos, axis=1, keepdims=True))).astype(jnp.bfloat16)
        pooled = jnp.einsum('tvh,vtd->thd', weights.astype(jnp.float32), embedded.astype(jnp.float32)).astype(jnp.bfloat16)
        place_rows = lax.dynamic_slice_in_dim(position, start_row, BAND_TOK, 0)
        merged = jnp.einsum('thd,dhe->the', pooled.astype(jnp.float32), value_heads).reshape(BAND_TOK, D) + place_rows.astype(jnp.float32)
        normed = normalize(merged).astype(jnp.bfloat16)
        qkv = jnp.einsum('td,dcf->tcf', normed.astype(jnp.float32), qkv_weight.astype(jnp.float32)).astype(jnp.bfloat16)
        return (merged, qkv)
    merged_all, qkv_all = lax.map(front, jnp.arange(N_BAND, dtype=jnp.int32))
    scale = HEAD_DIM ** (-0.5)

    def attend(band_index):
        offsets = jnp.arange(-REACH, REACH + 1, dtype=jnp.int32)
        seen = ((band_index + offsets + N_BAND) % N_BAND).astype(jnp.int32)
        query_heads = qkv_all[band_index, :, 0].astype(jnp.float32).reshape(BAND_TOK, HEADS, HEAD_DIM)
        key_heads = qkv_all[seen, :, 1].astype(jnp.float32).reshape(-1, HEADS, HEAD_DIM)
        val_heads = qkv_all[seen, :, 2].astype(jnp.float32).reshape(-1, HEADS, HEAD_DIM)
        scores = jnp.einsum('thd,shd->hts', query_heads, key_heads) * scale
        expos = jnp.exp(scores)
        denom = lax.optimization_barrier(jnp.sum(expos, axis=-1))
        numer = jnp.einsum('hts,shd->thd', expos.astype(jnp.bfloat16).astype(jnp.float32), val_heads)
        context = (numer / jnp.transpose(denom)[:, :, None]).astype(jnp.bfloat16).reshape(BAND_TOK, D)
        return jnp.dot(context, out_weight, preferred_element_type=jnp.float32)
    update = lax.map(attend, jnp.arange(N_BAND, dtype=jnp.int32))
    return (merged_all + update).reshape(TOKENS, D).astype(jnp.bfloat16)
```

```python
import functools

import jax
import jax.numpy as jnp
from jax import lax
from jax.experimental import pallas as pl
from jax.experimental.pallas import tpu as pltpu
from jax.sharding import PartitionSpec as P

HEAD_DIM = 64
EPSILON = 1e-05
F32 = jnp.float32
BF16 = jnp.bfloat16
NT = (((1,), (1,)), ((), ()))
NN = (((1,), (0,)), ((), ()))


def dot(a, b, dims=NN):
    return lax.dot_general(a, b, dims, preferred_element_type=F32)


def shifted(block, axis, distance):
    n = lax.axis_size(axis)
    return lax.ppermute(block, axis, [((i + distance) % n, i) for i in range(n)])


def call(body, outs, args, flops, name):
    nbytes = sum(a.size * a.dtype.itemsize for a in (*args, *outs))
    return pl.pallas_call(
        body,
        out_shape=outs,
        in_specs=[pl.BlockSpec(memory_space=pltpu.VMEM) for _ in args],
        out_specs=[pl.BlockSpec(memory_space=pltpu.VMEM) for _ in outs],
        compiler_params=pltpu.CompilerParams(vmem_limit_bytes=40 * 1024 * 1024),
        cost_estimate=pl.CostEstimate(flops=flops, bytes_accessed=nbytes, transcendentals=0),
        name=name,
    )(*args)


def fold(table, offsets, key_t, agg_value):
    values = jnp.transpose(dot(table, agg_value)).astype(BF16)
    offset_values = jnp.transpose(dot(offsets, agg_value)).astype(BF16)
    return values, offset_values, dot(key_t, table, NT), dot(key_t, offsets, NT)


def fold_body(table, offsets, key_t, agg_value, *outs):
    for out, part in zip(outs, fold(table[...], offsets[...], key_t[...], agg_value[...])):
        out[...] = part


def front(pix, values, offset_values, keys, offset_keys, position):
    n_heads, n_rows = keys.shape
    n_vars = offset_keys.shape[1]
    n_pix = n_rows // n_vars
    tok = pix.shape[1]
    rows = lax.broadcasted_iota(jnp.int32, (n_vars * n_heads, n_rows), 0) // n_heads
    cols = lax.broadcasted_iota(jnp.int32, (n_vars * n_heads, n_rows), 1) // n_pix
    spread = jnp.where(rows == cols, jnp.concatenate([keys] * n_vars, axis=0), 0.0)
    high = spread.astype(BF16)
    low = (spread - high.astype(F32)).astype(BF16)
    rows = lax.broadcasted_iota(jnp.int32, (n_vars * n_heads, n_vars), 0) // n_heads
    cols = lax.broadcasted_iota(jnp.int32, (n_vars * n_heads, n_vars), 1)
    base = jnp.sum(
        jnp.where(rows == cols, jnp.concatenate([offset_keys] * n_vars, axis=0), 0.0), axis=1, keepdims=True
    )
    scores = dot(high, pix) + dot(low, pix) + base
    expos = jnp.exp(scores).reshape(n_vars, n_heads, tok)
    weights = (expos / jnp.sum(expos, axis=0, keepdims=True)).astype(BF16).astype(F32)
    points = pix.astype(F32).reshape(n_vars, n_pix, tok)
    merged = []
    for h in range(n_heads):
        head = weights[:, h, :]
        mixed = (head[:, None, :] * points).reshape(n_rows, tok).astype(BF16)
        own = slice(h * HEAD_DIM, (h + 1) * HEAD_DIM)
        merged.append(dot(values[own], mixed) + dot(offset_values[own], head.astype(BF16)))
    merged = jnp.transpose(jnp.concatenate(merged, axis=0))
    return merged + position.astype(F32)


def project(merged, weight, qkv_out):
    centre = jnp.mean(merged, axis=-1, keepdims=True)
    centred = merged - centre
    spread = jnp.mean(jnp.square(centred), axis=-1, keepdims=True)
    normed = (centred * lax.rsqrt(spread + EPSILON)).astype(BF16)
    for c in range(3):
        qkv_out[c] = dot(normed, weight[c]).astype(BF16)


def tokens_of(pix_refs, distance, tok):
    n = len(pix_refs)
    me = lax.axis_index("var")
    start = pl.multiple_of(lax.rem(me + distance, n) * tok, tok)
    return jnp.concatenate([ref[:, pl.ds(start, tok)] for ref in pix_refs], axis=0)


def first_body(n, *refs):
    tables, offsets, pix, folded = refs[: n - 1], refs[n - 1 : 2 * n - 2], refs[2 * n - 2 : 3 * n - 2], refs[3 * n - 2 : 3 * n + 2]
    key_t, agg_value, position, weight = refs[3 * n + 2 : 3 * n + 6]
    values, offset_values, keys, offset_keys, merged_out, qkv_out = refs[3 * n + 6 :]
    parts = [tuple(ref[...] for ref in folded)]
    for table, offset in zip(tables, offsets):
        parts.append(fold(table[...], offset[...], key_t[...], agg_value[...]))
    for out, shares in zip((values, offset_values, keys, offset_keys), zip(*parts)):
        out[...] = jnp.concatenate(shares, axis=1)
    tok = position.shape[0]
    merged = front(
        tokens_of(pix, 0, tok), values[...], offset_values[...], keys[...], offset_keys[...], position[...]
    )
    merged_out[...] = merged
    project(merged, weight, qkv_out)


def later_body(n, distance, *refs):
    pix, (values, offset_values, keys, offset_keys, position, weight, qkv_out) = refs[:n], refs[n:]
    tok = position.shape[0]
    merged = front(
        tokens_of(pix, distance, tok), values[...], offset_values[...], keys[...], offset_keys[...], position[...]
    )
    project(merged, weight, qkv_out)


def attend(query, pairs):
    tok, width = query.shape
    group = min(width, 128)
    per = group // HEAD_DIM
    lanes = lax.broadcasted_iota(jnp.int32, (1, group), 1) // HEAD_DIM
    out = []
    for g in range(width // group):
        cut = slice(g * group, (g + 1) * group)
        block = query[:, cut]
        done = None
        for h in range(per):
            mine = jnp.where(lanes == h, block, jnp.zeros_like(block))
            numer, denom = 0.0, 0.0
            for pair in pairs:
                expos = jnp.exp(dot(mine, pair[0, :, cut], NT))
                denom = denom + jnp.sum(expos, axis=-1, keepdims=True)
                numer = numer + dot(expos.astype(BF16), pair[1, :, cut])
            head = numer / denom
            done = head if done is None else jnp.where(lanes == h, head, done)
        out.append(done.astype(BF16))
    return jnp.concatenate(out, axis=1)


def attend_body(*refs):
    qkv, pairs, out_weight, out = refs[0], refs[1:-2], refs[-2], refs[-1]
    scale = HEAD_DIM ** (-0.5)
    query = qkv[0] * jnp.asarray(scale, BF16)
    context = attend(query, pairs)
    out[...] = dot(context, out_weight[...]).astype(out.dtype)


def shards(pixels, embed_weight, variable_embed, agg_key, agg_value, position, qkv_weight, out_weight):
    n = lax.axis_size("var")
    n_vars, n_pix, band_tok = pixels.shape
    d = embed_weight.shape[2]
    tok = position.shape[0]
    width = qkv_weight.shape[2]
    n_heads = agg_key.shape[1]
    all_vars = n_vars * n
    rows = n_vars * n_pix
    table = embed_weight.reshape(rows, d)
    pix = pixels.reshape(rows, band_tok)
    key_t = jnp.transpose(agg_key)
    weight = jnp.transpose(qkv_weight, (1, 0, 2))

    tables = [shifted(table, "var", r) for r in range(1, n)]
    pixs = [pix] + [shifted(pix, "var", r) for r in range(1, n)]
    offsets = [shifted(variable_embed, "var", r) for r in range(1, n)]
    positions = [position] + [shifted(position, "var", r) for r in range(1, n)]

    sds = jax.ShapeDtypeStruct
    folded = call(
        fold_body,
        [sds((d, rows), BF16), sds((d, n_vars), BF16), sds((n_heads, rows), F32), sds((n_heads, n_vars), F32)],
        (table, variable_embed, key_t, agg_value),
        2 * (rows + n_vars) * d * (d + n_heads),
        "fold",
    )
    *weights, merged, own = call(
        functools.partial(first_body, n),
        [
            sds((d, rows * n), BF16),
            sds((d, all_vars), BF16),
            sds((n_heads, rows * n), F32),
            sds((n_heads, all_vars), F32),
            sds((tok, d), F32),
            sds((3, tok, width), BF16),
        ],
        (*tables, *offsets, *pixs, *folded, key_t, agg_value, position, weight),
        2 * (n - 1) * (rows + n_vars) * d * d + 2 * tok * d * (3 * width + 2 * rows),
        "front_own",
    )
    qkvs = [own]
    for r in range(1, n):
        qkvs += call(
            functools.partial(later_body, n, r),
            [sds((3, tok, width), BF16)],
            (*pixs, *weights, positions[r], weight),
            2 * tok * d * (3 * width + 2 * rows),
            "front_later",
        )
    pairs = [x[1:] for x in qkvs]
    pairs += [shifted(x, "band", 1) for x in pairs] + [shifted(x, "band", -1) for x in pairs[:n]]
    flops = 4 * tok * band_tok * 3 * width + 2 * tok * width * d
    update = None
    for r in range(1, n):
        (share,) = call(attend_body, [sds((tok, d), BF16)], (qkvs[r], *pairs, out_weight), flops, "attend")
        share = shifted(share, "var", n - r).astype(F32)
        update = share if update is None else update + share
    (share,) = call(attend_body, [sds((tok, d), F32)], (own, *pairs, out_weight), flops, "attend_own")
    update = share if update is None else update + share
    return (merged + update).astype(BF16)


def solution(mesh):
    in_specs = (
        P("var", None, "band"),
        P("var", None, None),
        P("var", None),
        P(),
        P(),
        P(("band", "var"), None),
        P(None, None, "var"),
        P("var", None),
    )
    out_specs = P(("band", "var"), None)
    return jax.shard_map(shards, mesh=mesh, in_specs=in_specs, out_specs=out_specs, check_vma=False)
```

```python
import functools

import jax
import jax.numpy as jnp
from jax import lax
from jax.experimental import pallas as pl
from jax.experimental.pallas import tpu as pltpu
from jax.sharding import PartitionSpec as P

HEAD_DIM = 64
EPSILON = 1e-05
F32 = jnp.float32
BF16 = jnp.bfloat16
NT = (((1,), (1,)), ((), ()))
NN = (((1,), (0,)), ((), ()))


def dot(a, b, dims=NN):
    return lax.dot_general(a, b, dims, preferred_element_type=F32)


def shifted(block, axis, distance):
    n = lax.axis_size(axis)
    return lax.ppermute(block, axis, [((i + distance) % n, i) for i in range(n)])


def paired(block):
    return lax.ppermute(block, "band", [(i ^ 1, i) for i in range(lax.axis_size("band"))])


def call(body, outs, args, flops, name, spaces=None, scratch=()):
    nbytes = sum(a.size * a.dtype.itemsize for a in (*args, *outs))
    spaces = spaces or [pltpu.VMEM] * len(args)
    return pl.pallas_call(
        body,
        out_shape=outs,
        in_specs=[pl.BlockSpec(memory_space=space) for space in spaces],
        out_specs=[pl.BlockSpec(memory_space=pltpu.VMEM) for _ in outs],
        scratch_shapes=scratch,
        compiler_params=pltpu.CompilerParams(vmem_limit_bytes=32 * 1024 * 1024),
        cost_estimate=pl.CostEstimate(flops=flops, bytes_accessed=nbytes, transcendentals=0),
        name=name,
    )(*args)


def fold(table, offsets, key_t, agg_value):
    values = jnp.transpose(dot(table, agg_value)).astype(BF16)
    offset_values = jnp.transpose(dot(offsets, agg_value)).astype(BF16)
    return values, offset_values, dot(key_t, table, NT), dot(key_t, offsets, NT)


def stage_body(n_in, *refs):
    sources, staged, folded, sems = refs[:n_in], refs[n_in : 2 * n_in], refs[2 * n_in : -1], refs[-1]
    copies = [pltpu.make_async_copy(a, b, sems.at[i]) for i, (a, b) in enumerate(zip(sources, staged))]
    for copy in copies:
        copy.start()
    for copy in copies[:4]:
        copy.wait()
    for out, part in zip(folded, fold(*(ref[...] for ref in staged[:4]))):
        out[...] = part
    for copy in copies[4:]:
        copy.wait()


def front(pix, values, offset_values, keys, offset_keys, position):
    n_heads, n_rows = keys.shape
    n_vars = offset_keys.shape[1]
    n_pix = n_rows // n_vars
    tok = pix.shape[1]
    rows = lax.broadcasted_iota(jnp.int32, (n_vars * n_heads, n_rows), 0) // n_heads
    cols = lax.broadcasted_iota(jnp.int32, (n_vars * n_heads, n_rows), 1) // n_pix
    spread = jnp.where(rows == cols, jnp.concatenate([keys] * n_vars, axis=0), 0.0)
    high = spread.astype(BF16)
    low = (spread - high.astype(F32)).astype(BF16)
    rows = lax.broadcasted_iota(jnp.int32, (n_vars * n_heads, n_vars), 0) // n_heads
    cols = lax.broadcasted_iota(jnp.int32, (n_vars * n_heads, n_vars), 1)
    base = jnp.sum(
        jnp.where(rows == cols, jnp.concatenate([offset_keys] * n_vars, axis=0), 0.0), axis=1, keepdims=True
    )
    scores = dot(high, pix) + dot(low, pix) + base
    expos = jnp.exp(scores).reshape(n_vars, n_heads, tok)
    weights = (expos / jnp.sum(expos, axis=0, keepdims=True)).astype(BF16).astype(F32)
    points = pix.astype(F32).reshape(n_vars, n_pix, tok)
    merged = []
    for h in range(n_heads):
        head = weights[:, h, :]
        mixed = (head[:, None, :] * points).reshape(n_rows, tok).astype(BF16)
        own = slice(h * HEAD_DIM, (h + 1) * HEAD_DIM)
        merged.append(dot(values[own], mixed) + dot(offset_values[own], head.astype(BF16)))
    merged = jnp.transpose(jnp.concatenate(merged, axis=0))
    return merged + position.astype(F32)


def project(merged, weight, query_out, pair_out):
    centre = jnp.mean(merged, axis=-1, keepdims=True)
    centred = merged - centre
    spread = jnp.mean(jnp.square(centred), axis=-1, keepdims=True)
    normed = (centred * lax.rsqrt(spread + EPSILON)).astype(BF16)
    query_out[...] = (dot(normed, weight[0]).astype(BF16) * HEAD_DIM ** (-0.5)).astype(BF16)
    for c in range(2):
        pair_out[c] = dot(normed, weight[c + 1]).astype(BF16)


def tokens_of(pix_refs, distance, tok):
    n = len(pix_refs)
    me = lax.axis_index("var")
    start = pl.multiple_of(lax.rem(me + distance, n) * tok, tok)
    return jnp.concatenate([ref[:, pl.ds(start, tok)] for ref in pix_refs], axis=0)


def first_body(n, *refs):
    near, far, pix, folded = (refs[i : i + k] for i, k in ((0, n - 1), (n - 1, n - 1), (2 * n - 2, n), (3 * n - 2, 4)))
    key_t, agg_value, position, weight = refs[3 * n + 2 : 3 * n + 6]
    values, offset_values, keys, offset_keys, merged_out, query_out, pair_out, table = refs[3 * n + 6 :]
    half = table.shape[0] // 2
    side = lax.rem(lax.axis_index("band"), 2)
    parts = [tuple(ref[...] for ref in folded)]
    for mine, other in zip(near, far):
        table[pl.ds(pl.multiple_of(side * half, half), half)] = mine[:half]
        table[pl.ds(pl.multiple_of((1 - side) * half, half), half)] = other[:half]
        parts.append(fold(table[...], mine[half:], key_t[...], agg_value[...]))
    for out, shares in zip((values, offset_values, keys, offset_keys), zip(*parts)):
        out[...] = jnp.concatenate(shares, axis=1)
    tok = position.shape[0]
    merged = front(
        tokens_of(pix, 0, tok), values[...], offset_values[...], keys[...], offset_keys[...], position[...]
    )
    merged_out[...] = merged
    project(merged, weight, query_out, pair_out)


def later_body(n, distance, *refs):
    pix, (values, offset_values, keys, offset_keys, position, weight), rest = refs[:n], refs[n : n + 6], refs[n + 6 :]
    earlier, query_out, pair_out = rest[:-2], rest[-2], rest[-1]
    tok = position.shape[0]
    merged = front(
        tokens_of(pix, distance, tok), values[...], offset_values[...], keys[...], offset_keys[...], position[...]
    )
    for i, pair in enumerate(earlier):
        pair_out[:, i * tok : (i + 1) * tok] = pair[...]
    project(merged, weight, query_out, pair_out.at[:, pl.ds(len(earlier) * tok, tok)])


def absorb(query, pairs):
    tok, width = query.shape
    group = min(width, 128)
    per = group // HEAD_DIM
    lanes = lax.broadcasted_iota(jnp.int32, (1, group), 1) // HEAD_DIM
    numers, denoms = [], []
    for g in range(width // group):
        cut = slice(g * group, (g + 1) * group)
        block = query[:, cut]
        stack = jnp.concatenate([jnp.where(lanes == h, block, jnp.zeros_like(block)) for h in range(per)], axis=0)
        numer, denom = 0.0, 0.0
        for pair in pairs:
            expos = jnp.exp(dot(stack, pair[0, :, cut], NT))
            denom = denom + jnp.sum(expos, axis=-1, keepdims=True)
            numer = numer + dot(expos.astype(BF16), pair[1, :, cut])
        denom = jnp.broadcast_to(denom, numer.shape)
        top, low = numer[:tok], denom[:tok]
        for h in range(1, per):
            top = jnp.where(lanes == h, numer[h * tok : (h + 1) * tok], top)
            low = jnp.where(lanes == h, denom[h * tok : (h + 1) * tok], low)
        numers.append(top)
        denoms.append(low)
    return jnp.concatenate(numers, axis=1), jnp.concatenate(denoms, axis=1)


def begin_body(n, *refs):
    queries, pair, totals = refs[:n], refs[n], refs[n + 1 :]
    for i, query in enumerate(queries):
        totals[2 * i][...], totals[2 * i + 1][...] = absorb(query[...], [pair])


def finish_body(query, numer, denom, east, west, out_weight, *refs):
    top, low = absorb(query[...], [east, west])
    context = ((numer[...] + top) / (denom[...] + low)).astype(BF16)
    update = dot(context, out_weight[...])
    out = refs[-1]
    for ref in refs[:-1]:
        update = update + ref[...]
    out[...] = update.astype(out.dtype)


def shards(pixels, embed_weight, variable_embed, agg_key, agg_value, position, qkv_weight, out_weight):
    n = lax.axis_size("var")
    n_vars, n_pix, band_tok = pixels.shape
    d = embed_weight.shape[2]
    tok = position.shape[0]
    width = qkv_weight.shape[2]
    n_heads = agg_key.shape[1]
    all_vars = n_vars * n
    rows = n_vars * n_pix
    sds = jax.ShapeDtypeStruct
    table = embed_weight.reshape(rows, d)
    pix = pixels.reshape(rows, band_tok)
    key_t = jnp.transpose(agg_key)
    weight = jnp.transpose(qkv_weight, (1, 0, 2))

    pixs = [shifted(pix, "var", r) for r in range(1, n)]
    side = lax.rem(lax.axis_index("band"), 2)
    half = jnp.concatenate([lax.dynamic_slice_in_dim(table, side * (rows // 2), rows // 2, 0), variable_embed], axis=0)
    near = [shifted(half, "var", r) for r in range(1, n)]
    positions = [shifted(position, "var", r) for r in range(1, n)]
    far = [paired(x) for x in near]

    moved = (table, variable_embed, key_t, agg_value, pix, position, weight, out_weight)
    *staged, f0, f1, f2, f3 = call(
        functools.partial(stage_body, len(moved)),
        [sds(a.shape, a.dtype) for a in moved]
        + [sds((d, rows), BF16), sds((d, n_vars), BF16), sds((n_heads, rows), F32), sds((n_heads, n_vars), F32)],
        moved,
        2 * (rows + n_vars) * d * (d + n_heads),
        "stage",
        [pl.ANY] * len(moved),
        [pltpu.SemaphoreType.DMA((len(moved),))],
    )
    _, _, key_t, agg_value, pix, position, weight, out_weight = staged
    pixs = [pix] + pixs
    front_flops = 2 * tok * d * (3 * width + 2 * rows)
    *folded, merged, query, pair = call(
        functools.partial(first_body, n),
        [
            sds((d, rows * n), BF16),
            sds((d, all_vars), BF16),
            sds((n_heads, rows * n), F32),
            sds((n_heads, all_vars), F32),
            sds((tok, d), F32),
            sds((tok, width), BF16),
            sds((2, tok, width), BF16),
        ],
        (*near, *far, *pixs, f0, f1, f2, f3, key_t, agg_value, position, weight),
        2 * (n - 1) * (rows + n_vars) * d * d + front_flops,
        "front_own",
        scratch=[pltpu.VMEM((rows, d), BF16)],
    )
    queries, pairs = [query], [pair]
    for r in range(1, n):
        last = r == n - 1
        query, pair = call(
            functools.partial(later_body, n, r),
            [sds((tok, width), BF16), sds((2, band_tok if last else tok, width), BF16)],
            (*pixs, *folded, positions[r - 1], weight, *(pairs if last else ())),
            front_flops,
            "front_later",
        )
        queries.append(query)
        pairs.append(pair)
    pair = pairs[-1]
    east, west = shifted(pair, "band", 1), shifted(pair, "band", -1)
    flops = 4 * tok * band_tok * width
    totals = call(
        functools.partial(begin_body, n),
        [sds((tok, width), F32)] * (2 * n),
        (*queries, pair),
        n * flops,
        "attend_band",
    )
    flops = 2 * flops + 2 * tok * width * d
    ending = []
    for r in range(1, n):
        (share,) = call(
            finish_body,
            [sds((tok, d), BF16)],
            (queries[r], *totals[2 * r : 2 * r + 2], east, west, out_weight),
            flops,
            "attend_later",
        )
        ending.append(shifted(share, "var", n - r))
    (update,) = call(
        finish_body,
        [sds((tok, d), F32)],
        (queries[0], *totals[:2], east, west, out_weight, merged),
        flops,
        "attend_own",
    )
    for share in ending:
        update = update + share.astype(F32)
    return update.astype(BF16)


def solution(mesh):
    in_specs = (
        P("var", None, "band"),
        P("var", None, None),
        P("var", None),
        P(),
        P(),
        P(("band", "var"), None),
        P(None, None, "var"),
        P("var", None),
    )
    out_specs = P(("band", "var"), None)
    return jax.shard_map(shards, mesh=mesh, in_specs=in_specs, out_specs=out_specs, check_vma=False)
```

```python
import functools

import jax
import jax.numpy as jnp
from jax import lax
from jax.experimental import pallas as pl
from jax.experimental.pallas import tpu as pltpu
from jax.sharding import PartitionSpec as P

HEAD_DIM = 64
EPSILON = 1e-05
F32 = jnp.float32
BF16 = jnp.bfloat16
NT = (((1,), (1,)), ((), ()))
NN = (((1,), (0,)), ((), ()))


def dot(a, b, dims=NN):
    return lax.dot_general(a, b, dims, preferred_element_type=F32)


def shifted(block, axis, distance):
    n = lax.axis_size(axis)
    return lax.ppermute(block, axis, [((i + distance) % n, i) for i in range(n)])


def inward(block):
    return lax.ppermute(block, "band", [(i ^ 1, i) for i in range(lax.axis_size("band"))])


def outward(block):
    n = lax.axis_size("band")
    return lax.ppermute(block, "band", [(i, (i + 1 if i % 2 else i - 1) % n) for i in range(n)])


def call(body, outs, args, flops, name, spaces=None, scratch=()):
    spaces = spaces or [pltpu.VMEM] * len(args)
    args = [pltpu.with_memory_space_constraint(a, s) if s == pltpu.HBM else a for a, s in zip(args, spaces)]
    return pl.pallas_call(
        body,
        out_shape=outs,
        in_specs=[pl.BlockSpec(memory_space=space) for space in spaces],
        out_specs=[pl.BlockSpec(memory_space=pltpu.VMEM) for _ in outs],
        scratch_shapes=scratch,
        compiler_params=pltpu.CompilerParams(vmem_limit_bytes=32 * 1024 * 1024),
        cost_estimate=pl.CostEstimate(flops=0, bytes_accessed=0, transcendentals=0),
        name=name,
    )(*args)


def fold(table, offsets, key_t, agg_value):
    values = jnp.transpose(dot(table, agg_value)).astype(BF16)
    offset_values = jnp.transpose(dot(offsets, agg_value)).astype(BF16)
    return values, offset_values, dot(key_t, table, NT), dot(key_t, offsets, NT)


def pack_body(table, offsets, pix, position, shared, placed, offsets_in, sems):
    rows, band_tok = pix.shape
    tok, d = position.shape
    half = table.shape[0] // 2
    blocks = d // band_tok
    depth = rows // blocks
    side = lax.rem(lax.axis_index("band"), 2)
    moves = [
        (offsets, offsets_in),
        (table.at[pl.ds(pl.multiple_of(side * half, half), half)], shared.at[pl.ds(depth, half)]),
        (position, placed.at[pl.ds(0, tok)]),
    ]
    for k in range(blocks):
        lanes = pl.ds(k * band_tok, band_tok)
        moves.append((pix.at[pl.ds(k * depth, depth)], shared.at[pl.ds(0, depth), lanes]))
        moves.append((pix.at[pl.ds(k * depth, depth)], placed.at[pl.ds(tok, depth), lanes]))
    copies = [pltpu.make_async_copy(a, b, sems.at[i]) for i, (a, b) in enumerate(moves)]
    for copy in copies:
        copy.start()
    for copy in copies:
        copy.wait()
    shared[depth + half :] = offsets_in[...]


def stage_body(n_in, *refs):
    sources, (table, offsets), staged = refs[:n_in], refs[-3:-1], refs[n_in : 2 * n_in - 2]
    folded, sems = refs[2 * n_in - 2 : -3], refs[-1]
    targets = [table, offsets, *staged]
    copies = [pltpu.make_async_copy(a, b, sems.at[i]) for i, (a, b) in enumerate(zip(sources, targets))]
    for copy in copies:
        copy.start()
    for copy in copies[:4]:
        copy.wait()
    for out, part in zip(folded, fold(*(ref[...] for ref in targets[:4]))):
        out[...] = part
    for copy in copies[4:]:
        copy.wait()


def front(pix, values, offset_values, keys, offset_keys, position):
    n_heads, n_rows = keys.shape
    n_vars = offset_keys.shape[1]
    n_pix = n_rows // n_vars
    tok = pix.shape[1]
    rows = lax.broadcasted_iota(jnp.int32, (n_vars * n_heads, n_rows), 0) // n_heads
    cols = lax.broadcasted_iota(jnp.int32, (n_vars * n_heads, n_rows), 1) // n_pix
    spread = jnp.where(rows == cols, jnp.concatenate([keys] * n_vars, axis=0), 0.0)
    high = spread.astype(BF16)
    low = (spread - high.astype(F32)).astype(BF16)
    rows = lax.broadcasted_iota(jnp.int32, (n_vars * n_heads, n_vars), 0) // n_heads
    cols = lax.broadcasted_iota(jnp.int32, (n_vars * n_heads, n_vars), 1)
    base = jnp.sum(
        jnp.where(rows == cols, jnp.concatenate([offset_keys] * n_vars, axis=0), 0.0), axis=1, keepdims=True
    )
    scores = dot(high, pix) + dot(low, pix) + base
    expos = jnp.exp(scores).reshape(n_vars, n_heads, tok)
    weights = (expos / jnp.sum(expos, axis=0, keepdims=True)).astype(BF16).astype(F32)
    points = pix.astype(F32).reshape(n_vars, n_pix, tok)
    merged = []
    for h in range(n_heads):
        head = weights[:, h, :]
        mixed = (head[:, None, :] * points).reshape(n_rows, tok).astype(BF16)
        own = slice(h * HEAD_DIM, (h + 1) * HEAD_DIM)
        merged.append(dot(values[own], mixed) + dot(offset_values[own], head.astype(BF16)))
    merged = jnp.transpose(jnp.concatenate(merged, axis=0))
    return merged + position.astype(F32)


def normalize(merged):
    centre = jnp.mean(merged, axis=-1, keepdims=True)
    centred = merged - centre
    spread = jnp.mean(jnp.square(centred), axis=-1, keepdims=True)
    return (centred * lax.rsqrt(spread + EPSILON)).astype(BF16)


def project(merged, weight, query_out, pair_out):
    normed = normalize(merged)
    query_out[...] = (dot(normed, weight[0]).astype(BF16) * HEAD_DIM ** (-0.5)).astype(BF16)
    for c in range(2):
        pair_out[c] = dot(normed, weight[c + 1]).astype(BF16)


def tokens_of(packs, first_row, distance, tok, depth, band_tok):
    start = lax.rem(lax.axis_index("var") + distance, len(packs)) * tok
    parts = []
    for ref in packs:
        for k in range(ref.shape[1] // band_tok):
            lanes = pl.ds(pl.multiple_of(k * band_tok + start, tok), tok)
            parts.append(ref[first_row : first_row + depth, lanes])
    return jnp.concatenate(parts, axis=0)


def first_body(n, depth, *refs):
    packs, far, folded = refs[:n], refs[n : 2 * n - 1], refs[2 * n - 1 : 2 * n + 3]
    key_t, agg_value, placed, weight = refs[2 * n + 3 : 2 * n + 7]
    values, offset_values, keys, offset_keys, merged_out, query_out, pair_out, table = refs[2 * n + 7 :]
    half = table.shape[0] // 2
    side = lax.rem(lax.axis_index("band"), 2)
    parts = [tuple(ref[...] for ref in folded)]
    for mine, other in zip(packs[1:], far):
        table[pl.ds(pl.multiple_of(side * half, half), half)] = mine[depth : depth + half]
        table[pl.ds(pl.multiple_of((1 - side) * half, half), half)] = other[depth : depth + half]
        parts.append(fold(table[...], mine[depth + half :], key_t[...], agg_value[...]))
    for out, shares in zip((values, offset_values, keys, offset_keys), zip(*parts)):
        out[...] = jnp.concatenate(shares, axis=1)
    tok = merged_out.shape[0]
    merged = front(
        tokens_of(packs, 0, 0, tok, depth, n * tok),
        values[...], offset_values[...], keys[...], offset_keys[...], placed[:tok],
    )
    merged_out[...] = merged
    project(merged, weight, query_out, pair_out)


def later_body(n, depth, distance, *refs):
    packs, (values, offset_values, keys, offset_keys, position, weight), rest = refs[:n], refs[n : n + 6], refs[n + 6 :]
    earlier, query_out, pair_out = rest[:-2], rest[-2], rest[-1]
    tok = position.shape[0]
    merged = front(
        tokens_of(packs, 0, distance, tok, depth, n * tok),
        values[...], offset_values[...], keys[...], offset_keys[...], position[...],
    )
    for i, pair in enumerate(earlier):
        pair_out[:, i * tok : (i + 1) * tok] = pair[...]
    project(merged, weight, query_out, pair_out.at[:, pl.ds(len(earlier) * tok, tok)])


def outer_body(n, depth, *refs):
    packs, (values, offset_values, keys, offset_keys, weight, pair_out) = refs[:n], refs[n:]
    tok = packs[0].shape[0] - depth
    step = min(n, 2)
    for r in range(0, n, step):
        pix = [tokens_of(packs, tok, r + i, tok, depth, n * tok) for i in range(step)]
        position = [packs[r + i][:tok] for i in range(step)]
        normed = normalize(
            front(
                jnp.concatenate(pix, axis=1),
                values[...], offset_values[...], keys[...], offset_keys[...], jnp.concatenate(position, axis=0),
            )
        )
        for c in range(2):
            pair_out[c, r * tok : (r + step) * tok] = dot(normed, weight[c + 1]).astype(BF16)


def absorb(query, pairs):
    tok, width = query.shape
    group = min(width, 128)
    per = group // HEAD_DIM
    lanes = lax.broadcasted_iota(jnp.int32, (1, group), 1) // HEAD_DIM
    numers, denoms = [], []
    for g in range(width // group):
        cut = slice(g * group, (g + 1) * group)
        block = query[:, cut]
        stack = jnp.concatenate([jnp.where(lanes == h, block, jnp.zeros_like(block)) for h in range(per)], axis=0)
        numer, denom = 0.0, 0.0
        for pair in pairs:
            expos = jnp.exp(dot(stack, pair[0, :, cut], NT))
            denom = denom + jnp.sum(expos, axis=-1, keepdims=True)
            numer = numer + dot(expos.astype(BF16), pair[1, :, cut])
        denom = jnp.broadcast_to(denom, numer.shape)
        top, low = numer[:tok], denom[:tok]
        for h in range(1, per):
            top = jnp.where(lanes == h, numer[h * tok : (h + 1) * tok], top)
            low = jnp.where(lanes == h, denom[h * tok : (h + 1) * tok], low)
        numers.append(top)
        denoms.append(low)
    return jnp.concatenate(numers, axis=1), jnp.concatenate(denoms, axis=1)


def begin_body(n, *refs):
    queries, pair, totals = refs[:n], refs[n], refs[n + 1 :]
    for i, query in enumerate(queries):
        totals[2 * i][...], totals[2 * i + 1][...] = absorb(query[...], [pair])


def finish_body(query, numer, denom, inner, outer, out_weight, *refs):
    top, low = absorb(query[...], [inner, outer])
    context = ((numer[...] + top) / (denom[...] + low)).astype(BF16)
    update = dot(context, out_weight[...])
    out = refs[-1]
    for ref in refs[:-1]:
        update = update + ref[...]
    out[...] = update.astype(out.dtype)


def shards(pixels, embed_weight, variable_embed, agg_key, agg_value, position, qkv_weight, out_weight):
    n = lax.axis_size("var")
    n_vars, n_pix, band_tok = pixels.shape
    d = embed_weight.shape[2]
    tok = position.shape[0]
    width = qkv_weight.shape[2]
    n_heads = agg_key.shape[1]
    all_vars = n_vars * n
    rows = n_vars * n_pix
    depth = rows * band_tok // d
    sds = jax.ShapeDtypeStruct
    table = embed_weight.reshape(rows, d)
    pix = pixels.reshape(rows, band_tok)
    key_t = jnp.transpose(agg_key)
    weight = jnp.transpose(qkv_weight, (1, 0, 2))

    shared, placed = call(
        pack_body,
        [sds((depth + rows // 2 + n_vars, d), BF16), sds((tok + depth, d), BF16)],
        (table, variable_embed, pix, position),
        0,
        "pack",
        [pltpu.HBM] * 4,
        [pltpu.VMEM((n_vars, d), BF16), pltpu.SemaphoreType.DMA((3 + 2 * (d // band_tok),))],
    )
    near = [shifted(shared, "var", r) for r in range(1, n)]
    outer = outward(placed)
    positions = [shifted(position, "var", r) for r in range(1, n)]

    moved = (table, variable_embed, key_t, agg_value, weight, out_weight)
    key_t, agg_value, weight, out_weight, *folded = call(
        functools.partial(stage_body, len(moved)),
        [sds(a.shape, a.dtype) for a in moved[2:]]
        + [sds((d, rows), BF16), sds((d, n_vars), BF16), sds((n_heads, rows), F32), sds((n_heads, n_vars), F32)],
        moved,
        2 * (rows + n_vars) * d * (d + n_heads),
        "stage",
        [pltpu.HBM] * len(moved),
        [pltpu.VMEM((rows, d), BF16), pltpu.VMEM((n_vars, d), BF16), pltpu.SemaphoreType.DMA((len(moved),))],
    )
    *near, _ = lax.optimization_barrier((*near, folded[2]))
    far = [inward(x) for x in near]
    packs = [shared] + near
    outer, _, *far = lax.optimization_barrier((outer, folded[0], *far))
    outers = [outer] + [shifted(outer, "var", r) for r in range(1, n)]
    front_flops = 2 * tok * d * (3 * width + 2 * rows)
    *folded, merged, query, pair = call(
        functools.partial(first_body, n, depth),
        [
            sds((d, rows * n), BF16),
            sds((d, all_vars), BF16),
            sds((n_heads, rows * n), F32),
            sds((n_heads, all_vars), F32),
            sds((tok, d), F32),
            sds((tok, width), BF16),
            sds((2, tok, width), BF16),
        ],
        (*packs, *far, *folded, key_t, agg_value, placed, weight),
        2 * (n - 1) * (rows + n_vars) * d * d + front_flops,
        "front_own",
        scratch=[pltpu.VMEM((rows, d), BF16)],
    )
    queries, pairs = [query], [pair]
    for r in range(1, n):
        last = r == n - 1
        query, pair = call(
            functools.partial(later_body, n, depth, r),
            [sds((tok, width), BF16), sds((2, band_tok if last else tok, width), BF16)],
            (*packs, *folded, positions[r - 1], weight, *(pairs if last else ())),
            front_flops,
            "front_later",
        )
        queries.append(query)
        pairs.append(pair)
    pair = pairs[-1]
    inner = inward(pair)
    flops = 4 * tok * band_tok * width
    totals = call(
        functools.partial(begin_body, n),
        [sds((tok, width), F32)] * (2 * n),
        (*queries, pair),
        n * flops,
        "attend_band",
    )
    *outers, _ = lax.optimization_barrier((*outers, totals[0]))
    (outer_pair,) = call(
        functools.partial(outer_body, n, depth),
        [sds((2, band_tok, width), BF16)],
        (*outers, *folded, weight),
        n * front_flops,
        "front_outer",
    )
    flops += 2 * tok * width * d
    ending = []
    for r in range(1, n):
        (share,) = call(
            finish_body,
            [sds((tok, d), BF16)],
            (queries[r], *totals[2 * r : 2 * r + 2], inner, outer_pair, out_weight),
            flops,
            "attend_later",
        )
        ending.append(shifted(share, "var", n - r))
    (update,) = call(
        finish_body,
        [sds((tok, d), F32)],
        (queries[0], *totals[:2], inner, outer_pair, out_weight, merged),
        flops,
        "attend_own",
    )
    for share in ending:
        update = update + share.astype(F32)
    return update.astype(BF16)


def solution(mesh):
    in_specs = (
        P("var", None, "band"),
        P("var", None, None),
        P("var", None),
        P(),
        P(),
        P(("band", "var"), None),
        P(None, None, "var"),
        P("var", None),
    )
    out_specs = P(("band", "var"), None)
    return jax.shard_map(shards, mesh=mesh, in_specs=in_specs, out_specs=out_specs, check_vma=False)
```

```python
import functools

import jax
import jax.numpy as jnp
from jax import lax
from jax.experimental import pallas as pl
from jax.experimental.pallas import tpu as pltpu
from jax.sharding import PartitionSpec as P

HEAD_DIM = 64
EPSILON = 1e-05
F32 = jnp.float32
BF16 = jnp.bfloat16
NT = (((1,), (1,)), ((), ()))
NN = (((1,), (0,)), ((), ()))


def dot(a, b, dims=NN):
    return lax.dot_general(a, b, dims, preferred_element_type=F32)


def shifted(block, axis, distance):
    n = lax.axis_size(axis)
    return lax.ppermute(block, axis, [((i + distance) % n, i) for i in range(n)])


def inward(block):
    return lax.ppermute(block, "band", [(i ^ 1, i) for i in range(lax.axis_size("band"))])


def outward(block):
    n = lax.axis_size("band")
    return lax.ppermute(block, "band", [(i, (i + 1 if i % 2 else i - 1) % n) for i in range(n)])


def call(body, outs, args, flops, name, spaces=None, scratch=()):
    spaces = spaces or [pltpu.VMEM] * len(args)
    args = [pltpu.with_memory_space_constraint(a, s) if s == pltpu.HBM else a for a, s in zip(args, spaces)]
    return pl.pallas_call(
        body,
        out_shape=outs,
        in_specs=[pl.BlockSpec(memory_space=space) for space in spaces],
        out_specs=[pl.BlockSpec(memory_space=pltpu.VMEM) for _ in outs],
        scratch_shapes=scratch,
        compiler_params=pltpu.CompilerParams(vmem_limit_bytes=32 * 1024 * 1024),
        cost_estimate=pl.CostEstimate(flops=20_000_000_000 if name == "attend_band" else 0, bytes_accessed=0, transcendentals=0),
        name=name,
    )(*args)


def fold(table, offsets, key_t, agg_value):
    values = jnp.transpose(dot(table, agg_value)).astype(BF16)
    offset_values = jnp.transpose(dot(offsets, agg_value)).astype(BF16)
    return values, offset_values, dot(key_t, table, NT), dot(key_t, offsets, NT)


def pack_body(table, offsets, pix, position, shared, placed, offsets_in, sems):
    rows, band_tok = pix.shape
    tok, d = position.shape
    half = table.shape[0] // 2
    blocks = d // band_tok
    depth = rows // blocks
    side = lax.rem(lax.axis_index("band"), 2)
    moves = [
        (offsets, offsets_in),
        (table.at[pl.ds(pl.multiple_of(side * half, half), half)], shared.at[pl.ds(depth, half)]),
        (position, placed.at[pl.ds(0, tok)]),
    ]
    for k in range(blocks):
        lanes = pl.ds(k * band_tok, band_tok)
        moves.append((pix.at[pl.ds(k * depth, depth)], shared.at[pl.ds(0, depth), lanes]))
        moves.append((pix.at[pl.ds(k * depth, depth)], placed.at[pl.ds(tok, depth), lanes]))
    copies = [pltpu.make_async_copy(a, b, sems.at[i]) for i, (a, b) in enumerate(moves)]
    for copy in copies:
        copy.start()
    for copy in copies:
        copy.wait()
    shared[depth + half :] = offsets_in[...]


def stage_body(n_in, *refs):
    sources, (table, offsets), staged = refs[:n_in], refs[-3:-1], refs[n_in : 2 * n_in - 2]
    folded, sems = refs[2 * n_in - 2 : -3], refs[-1]
    targets = [table, offsets, *staged]
    copies = [pltpu.make_async_copy(a, b, sems.at[i]) for i, (a, b) in enumerate(zip(sources, targets))]
    for copy in copies:
        copy.start()
    for copy in copies[:4]:
        copy.wait()
    for out, part in zip(folded, fold(*(ref[...] for ref in targets[:4]))):
        out[...] = part
    for copy in copies[4:]:
        copy.wait()


def front(pix, values, offset_values, keys, offset_keys, position):
    n_heads, n_rows = keys.shape
    n_vars = offset_keys.shape[1]
    n_pix = n_rows // n_vars
    tok = pix.shape[1]
    rows = lax.broadcasted_iota(jnp.int32, (n_vars * n_heads, n_rows), 0) // n_heads
    cols = lax.broadcasted_iota(jnp.int32, (n_vars * n_heads, n_rows), 1) // n_pix
    spread = jnp.where(rows == cols, jnp.concatenate([keys] * n_vars, axis=0), 0.0)
    high = spread.astype(BF16)
    low = (spread - high.astype(F32)).astype(BF16)
    rows = lax.broadcasted_iota(jnp.int32, (n_vars * n_heads, n_vars), 0) // n_heads
    cols = lax.broadcasted_iota(jnp.int32, (n_vars * n_heads, n_vars), 1)
    base = jnp.sum(
        jnp.where(rows == cols, jnp.concatenate([offset_keys] * n_vars, axis=0), 0.0), axis=1, keepdims=True
    )
    scores = dot(high, pix) + dot(low, pix) + base
    expos = jnp.exp(scores).reshape(n_vars, n_heads, tok)
    weights = (expos / jnp.sum(expos, axis=0, keepdims=True)).astype(BF16).astype(F32)
    points = pix.astype(F32).reshape(n_vars, n_pix, tok)
    merged = []
    for h in range(n_heads):
        head = weights[:, h, :]
        mixed = (head[:, None, :] * points).reshape(n_rows, tok).astype(BF16)
        own = slice(h * HEAD_DIM, (h + 1) * HEAD_DIM)
        merged.append(dot(values[own], mixed) + dot(offset_values[own], head.astype(BF16)))
    merged = jnp.transpose(jnp.concatenate(merged, axis=0))
    return merged + position.astype(F32)


def normalize(merged):
    centre = jnp.mean(merged, axis=-1, keepdims=True)
    centred = merged - centre
    spread = jnp.mean(jnp.square(centred), axis=-1, keepdims=True)
    return (centred * lax.rsqrt(spread + EPSILON)).astype(BF16)


def tokens_of(packs, first_row, distance, tok, depth, band_tok):
    start = lax.rem(lax.axis_index("var") + distance, len(packs)) * tok
    parts = []
    for ref in packs:
        for k in range(ref.shape[1] // band_tok):
            lanes = pl.ds(pl.multiple_of(k * band_tok + start, tok), tok)
            parts.append(ref[first_row : first_row + depth, lanes])
    return jnp.concatenate(parts, axis=0)


def band_body(n, depth, *refs):
    packs, far, folded = refs[:n], refs[n : 2 * n - 1], refs[2 * n - 1 : 2 * n + 3]
    positions, (key_t, agg_value, weight) = refs[2 * n + 3 : 3 * n + 3], refs[3 * n + 3 : 3 * n + 6]
    values, offset_values, keys, offset_keys, merged_out, query_out, pair_out, table = refs[3 * n + 6 :]
    half = table.shape[0] // 2
    side = lax.rem(lax.axis_index("band"), 2)
    parts = [tuple(ref[...] for ref in folded)]
    for mine, other in zip(packs[1:], far):
        table[pl.ds(pl.multiple_of(side * half, half), half)] = mine[depth : depth + half]
        table[pl.ds(pl.multiple_of((1 - side) * half, half), half)] = other[depth : depth + half]
        parts.append(fold(table[...], mine[depth + half :], key_t[...], agg_value[...]))
    for out, shares in zip((values, offset_values, keys, offset_keys), zip(*parts)):
        out[...] = jnp.concatenate(shares, axis=1)
    tok = merged_out.shape[0]
    step = min(n, 2)
    for r in range(0, n, step):
        pix = [tokens_of(packs, 0, r + i, tok, depth, n * tok) for i in range(step)]
        position = [positions[r + i][:tok] for i in range(step)]
        merged = front(
            jnp.concatenate(pix, axis=1),
            values[...], offset_values[...], keys[...], offset_keys[...], jnp.concatenate(position, axis=0),
        )
        if r == 0:
            merged_out[...] = merged[:tok]
        normed = normalize(merged)
        rows = slice(r * tok, (r + step) * tok)
        query_out[rows] = (dot(normed, weight[0]).astype(BF16) * HEAD_DIM ** (-0.5)).astype(BF16)
        for c in range(2):
            pair_out[c, rows] = dot(normed, weight[c + 1]).astype(BF16)


def outer_body(n, depth, *refs):
    packs, (values, offset_values, keys, offset_keys, weight) = refs[:n], refs[n : n + 5]
    query, numer, denom, inner, out_weight, pair_out, *share = refs[n + 5 :]
    tok = packs[0].shape[0] - depth
    step = min(n, 2)
    for r in range(0, n, step):
        pix = [tokens_of(packs, tok, r + i, tok, depth, n * tok) for i in range(step)]
        position = [packs[r + i][:tok] for i in range(step)]
        normed = normalize(
            front(
                jnp.concatenate(pix, axis=1),
                values[...], offset_values[...], keys[...], offset_keys[...], jnp.concatenate(position, axis=0),
            )
        )
        for c in range(2):
            pair_out[c, r * tok : (r + step) * tok] = dot(normed, weight[c + 1]).astype(BF16)
    if share:
        finish_body(1, query, numer, denom, inner, pair_out, out_weight, share[0])


def absorb(query, pairs):
    tok, width = query.shape
    group = min(width, 128)
    per = group // HEAD_DIM
    lanes = lax.broadcasted_iota(jnp.int32, (1, group), 1) // HEAD_DIM
    numers, denoms = [], []
    for g in range(width // group):
        cut = slice(g * group, (g + 1) * group)
        block = query[:, cut]
        stack = jnp.concatenate([jnp.where(lanes == h, block, jnp.zeros_like(block)) for h in range(per)], axis=0)
        numer, denom = 0.0, 0.0
        for pair in pairs:
            expos = jnp.exp(dot(stack, pair[0, :, cut], NT))
            denom = denom + jnp.sum(expos, axis=-1, keepdims=True)
            numer = numer + dot(expos.astype(BF16), pair[1, :, cut])
        denom = jnp.broadcast_to(denom, numer.shape)
        top, low = numer[:tok], denom[:tok]
        for h in range(1, per):
            top = jnp.where(lanes == h, numer[h * tok : (h + 1) * tok], top)
            low = jnp.where(lanes == h, denom[h * tok : (h + 1) * tok], low)
        numers.append(top)
        denoms.append(low)
    return jnp.concatenate(numers, axis=1), jnp.concatenate(denoms, axis=1)


def begin_body(query, pair, numer, denom):
    for r in range(0, query.shape[0], 256):
        rows = slice(r, r + 256)
        numer[rows], denom[rows] = absorb(query[rows], [pair])


def finish_body(distance, query, numer, denom, inner, outer, out_weight, *refs):
    out = refs[-1]
    tok = out.shape[0]
    rows = slice(distance * tok, (distance + 1) * tok)
    top, low = absorb(query[rows], [inner, outer])
    context = ((numer[rows] + top) / (denom[rows] + low)).astype(BF16)
    update = dot(context, out_weight[...])
    for ref in refs[:-1]:
        update = update + ref[...]
    out[...] = update.astype(out.dtype)


def shards(pixels, embed_weight, variable_embed, agg_key, agg_value, position, qkv_weight, out_weight):
    n = lax.axis_size("var")
    n_vars, n_pix, band_tok = pixels.shape
    d = embed_weight.shape[2]
    tok = position.shape[0]
    width = qkv_weight.shape[2]
    n_heads = agg_key.shape[1]
    all_vars = n_vars * n
    rows = n_vars * n_pix
    depth = rows * band_tok // d
    sds = jax.ShapeDtypeStruct
    table = embed_weight.reshape(rows, d)
    pix = pixels.reshape(rows, band_tok)
    key_t = jnp.transpose(agg_key)
    weight = jnp.transpose(qkv_weight, (1, 0, 2))

    shared, placed = call(
        pack_body,
        [sds((depth + rows // 2 + n_vars, d), BF16), sds((tok + depth, d), BF16)],
        (table, variable_embed, pix, position),
        0,
        "pack",
        [pltpu.HBM] * 4,
        [pltpu.VMEM((n_vars, d), BF16), pltpu.SemaphoreType.DMA((3 + 2 * (d // band_tok),))],
    )
    near = [shifted(shared, "var", r) for r in range(1, n)]
    outer = outward(placed)
    positions = [shifted(position, "var", r) for r in range(1, n)]

    moved = (table, variable_embed, key_t, agg_value, weight, out_weight)
    key_t, agg_value, weight, out_weight, *folded = call(
        functools.partial(stage_body, len(moved)),
        [sds(a.shape, a.dtype) for a in moved[2:]]
        + [sds((d, rows), BF16), sds((d, n_vars), BF16), sds((n_heads, rows), F32), sds((n_heads, n_vars), F32)],
        moved,
        2 * (rows + n_vars) * d * (d + n_heads),
        "stage",
        [pltpu.HBM] * len(moved),
        [pltpu.VMEM((rows, d), BF16), pltpu.VMEM((n_vars, d), BF16), pltpu.SemaphoreType.DMA((len(moved),))],
    )
    *near, _ = lax.optimization_barrier((*near, folded[2]))
    far = [inward(x) for x in near]
    packs = [shared] + near
    outer, _, *far = lax.optimization_barrier((outer, folded[0], *far))
    outers = [outer] + [shifted(outer, "var", r) for r in range(1, n)]
    front_flops = 2 * band_tok * d * (3 * width + 2 * rows)
    *folded, merged, query, pair = call(
        functools.partial(band_body, n, depth),
        [
            sds((d, rows * n), BF16),
            sds((d, all_vars), BF16),
            sds((n_heads, rows * n), F32),
            sds((n_heads, all_vars), F32),
            sds((tok, d), F32),
            sds((band_tok, width), BF16),
            sds((2, band_tok, width), BF16),
        ],
        (*packs, *far, *folded, placed, *positions, key_t, agg_value, weight),
        2 * (n - 1) * (rows + n_vars) * d * d + front_flops,
        "front_band",
        scratch=[pltpu.VMEM((rows, d), BF16)],
    )
    inner = inward(pair)
    flops = 4 * tok * band_tok * width
    totals = call(begin_body, [sds((band_tok, width), F32)] * 2, (query, pair), n * flops, "attend_band")
    *outers, _ = lax.optimization_barrier((*outers, totals[0]))
    flops = 2 * flops + 2 * tok * width * d
    outer_pair, *share = call(
        functools.partial(outer_body, n, depth),
        [sds((2, band_tok, width), BF16)] + [sds((tok, d), BF16)] * (n > 1),
        (*outers, *folded, weight, query, *totals, inner, out_weight),
        front_flops + flops,
        "front_outer",
    )
    attended = (query, *totals, inner, outer_pair, out_weight)
    for r in range(2, n):
        share += call(functools.partial(finish_body, r), [sds((tok, d), BF16)], attended, flops, "attend_later")
    ending = [shifted(x, "var", n - r) for r, x in enumerate(share, 1)]
    (update,) = call(
        functools.partial(finish_body, 0), [sds((tok, d), F32)], (*attended, merged), flops, "attend_own"
    )
    for x in ending:
        update = update + x.astype(F32)
    return update.astype(BF16)


def solution(mesh):
    in_specs = (
        P("var", None, "band"),
        P("var", None, None),
        P("var", None),
        P(),
        P(),
        P(("band", "var"), None),
        P(None, None, "var"),
        P("var", None),
    )
    out_specs = P(("band", "var"), None)
    return jax.shard_map(shards, mesh=mesh, in_specs=in_specs, out_specs=out_specs, check_vma=False)
```

```python
import functools

import jax
import jax.numpy as jnp
from jax import lax
from jax.experimental import pallas as pl
from jax.experimental.pallas import tpu as pltpu
from jax.sharding import PartitionSpec as P

HEAD_DIM = 64
EPSILON = 1e-05
F32 = jnp.float32
BF16 = jnp.bfloat16
NT = (((1,), (1,)), ((), ()))
NN = (((1,), (0,)), ((), ()))


def dot(a, b, dims=NN):
    return lax.dot_general(a, b, dims, preferred_element_type=F32)


def shifted(block, axis, distance):
    n = lax.axis_size(axis)
    return lax.ppermute(block, axis, [((i + distance) % n, i) for i in range(n)])


def inward(block):
    return lax.ppermute(block, "band", [(i ^ 1, i) for i in range(lax.axis_size("band"))])


def outward(block):
    n = lax.axis_size("band")
    return lax.ppermute(block, "band", [(i, (i + 1 if i % 2 else i - 1) % n) for i in range(n)])


COST = {"mix_outer": 20.0, "front_band": 0.3}


def call(body, outs, args, name, spaces=None, scratch=()):
    spaces = spaces or [pltpu.VMEM] * len(args)
    args = [pltpu.with_memory_space_constraint(a, s) if s == pltpu.HBM else a for a, s in zip(args, spaces)]
    return pl.pallas_call(
        body,
        out_shape=outs,
        in_specs=[pl.BlockSpec(memory_space=space) for space in spaces],
        out_specs=[pl.BlockSpec(memory_space=pltpu.VMEM) for _ in outs],
        scratch_shapes=scratch,
        compiler_params=pltpu.CompilerParams(vmem_limit_bytes=32 * 1024 * 1024),
        cost_estimate=pl.CostEstimate(flops=int(COST.get(name, 0.0) * 1e9), bytes_accessed=0, transcendentals=0),
        name=name,
    )(*args)


def fold(table, offsets, key_t, agg_value):
    values = jnp.transpose(dot(table, agg_value)).astype(BF16)
    offset_values = jnp.transpose(dot(offsets, agg_value)).astype(BF16)
    return values, offset_values, dot(key_t, table, NT), dot(key_t, offsets, NT)


def pack_body(table, offsets, pix, position, half_out, shared, first, second, offsets_in, sems):
    rows, band_tok = pix.shape
    tok, d = position.shape
    half = table.shape[0] // 2
    blocks = d // band_tok
    depth = rows // blocks
    cut = first.shape[0] - depth
    side = lax.rem(lax.axis_index("band"), 2)
    moves = [
        (offsets, offsets_in),
        (table.at[pl.ds(pl.multiple_of(side * half, half), half)], half_out),
        (position, shared.at[pl.ds(depth, tok)]),
        (position.at[pl.ds(0, cut)], first.at[pl.ds(depth, cut)]),
        (position.at[pl.ds(cut, tok - cut)], second),
    ]
    for k in range(blocks):
        lanes = pl.ds(k * band_tok, band_tok)
        moves.append((pix.at[pl.ds(k * depth, depth)], shared.at[pl.ds(0, depth), lanes]))
        moves.append((pix.at[pl.ds(k * depth, depth)], first.at[pl.ds(0, depth), lanes]))
    copies = [pltpu.make_async_copy(a, b, sems.at[i]) for i, (a, b) in enumerate(moves)]
    for copy in copies:
        copy.start()
    for copy in copies:
        copy.wait()
    shared[depth + tok :] = offsets_in[...]


def stage_body(n_in, *refs):
    sources, (table, offsets), staged = refs[:n_in], refs[-3:-1], refs[n_in : 2 * n_in - 2]
    folded, sems = refs[2 * n_in - 2 : -3], refs[-1]
    targets = [table, offsets, *staged]
    copies = [pltpu.make_async_copy(a, b, sems.at[i]) for i, (a, b) in enumerate(zip(sources, targets))]
    for copy in copies:
        copy.start()
    for copy in copies[:4]:
        copy.wait()
    for out, part in zip(folded, fold(*(ref[...] for ref in targets[:4]))):
        out[...] = part
    for copy in copies[4:]:
        copy.wait()


def aggregate(pix, values, offset_values, keys, offset_keys):
    n_heads, n_rows = keys.shape
    n_vars = offset_keys.shape[1]
    n_pix = n_rows // n_vars
    tok = pix.shape[1]
    rows = lax.broadcasted_iota(jnp.int32, (n_vars * n_heads, n_rows), 0) // n_heads
    cols = lax.broadcasted_iota(jnp.int32, (n_vars * n_heads, n_rows), 1) // n_pix
    spread = jnp.where(rows == cols, jnp.concatenate([keys] * n_vars, axis=0), 0.0)
    high = spread.astype(BF16)
    low = (spread - high.astype(F32)).astype(BF16)
    rows = lax.broadcasted_iota(jnp.int32, (n_vars * n_heads, n_vars), 0) // n_heads
    cols = lax.broadcasted_iota(jnp.int32, (n_vars * n_heads, n_vars), 1)
    base = jnp.sum(
        jnp.where(rows == cols, jnp.concatenate([offset_keys] * n_vars, axis=0), 0.0), axis=1, keepdims=True
    )
    scores = dot(high, pix) + dot(low, pix) + base
    expos = jnp.exp(scores).reshape(n_vars, n_heads, tok)
    weights = (expos / jnp.sum(expos, axis=0, keepdims=True)).astype(BF16).astype(F32)
    points = pix.astype(F32).reshape(n_vars, n_pix, tok)
    merged = []
    for h in range(n_heads):
        head = weights[:, h, :]
        mixed = (head[:, None, :] * points).reshape(n_rows, tok).astype(BF16)
        own = slice(h * HEAD_DIM, (h + 1) * HEAD_DIM)
        merged.append(dot(values[own], mixed) + dot(offset_values[own], head.astype(BF16)))
    return jnp.transpose(jnp.concatenate(merged, axis=0))


def normalize(merged):
    centre = jnp.mean(merged, axis=-1, keepdims=True)
    centred = merged - centre
    spread = jnp.mean(jnp.square(centred), axis=-1, keepdims=True)
    return (centred * lax.rsqrt(spread + EPSILON)).astype(BF16)


def aggregates(packs, folded, tok, depth):
    n = len(packs)
    step = min(n, 2)
    for r in range(0, n, step):
        parts = []
        for ref in packs:
            for k in range(ref.shape[1] // (n * tok)):
                pieces = []
                for i in range(step):
                    start = k * n * tok + lax.rem(lax.axis_index("var") + r + i, n) * tok
                    pieces.append(ref[:depth, pl.ds(pl.multiple_of(start, tok), tok)])
                parts.append(jnp.concatenate(pieces, axis=1))
        pix = jnp.concatenate(parts, axis=0)
        yield slice(r * tok, (r + step) * tok), aggregate(pix, *(ref[...] for ref in folded))


def band_body(n, depth, *refs):
    packs, near, far, mine = refs[:n], refs[n : 2 * n - 1], refs[2 * n - 1 : 3 * n - 2], refs[3 * n - 2 : 3 * n + 2]
    key_t, agg_value, weight, *folded, merged_out, query_out, pair_out, table = refs[3 * n + 2 :]
    tok = merged_out.shape[0]
    half = table.shape[0] // 2
    side = lax.rem(lax.axis_index("band"), 2)
    parts = [tuple(ref[...] for ref in mine)]
    for pack, own, other in zip(packs[1:], near, far):
        table[pl.ds(pl.multiple_of(side * half, half), half)] = own[...]
        table[pl.ds(pl.multiple_of((1 - side) * half, half), half)] = other[...]
        parts.append(fold(table[...], pack[depth + tok :], key_t[...], agg_value[...]))
    for out, shares in zip(folded, zip(*parts)):
        out[...] = jnp.concatenate(shares, axis=1)
    for rows, merged in aggregates(packs, folded, tok, depth):
        spots = packs[rows.start // tok : rows.stop // tok]
        merged = merged + jnp.concatenate([ref[depth : depth + tok] for ref in spots], axis=0).astype(F32)
        if rows.start == 0:
            merged_out[...] = merged[:tok]
        normed = normalize(merged)
        query_out[rows] = (dot(normed, weight[0]).astype(BF16) * HEAD_DIM ** (-0.5)).astype(BF16)
        for c in range(2):
            pair_out[c, rows] = dot(normed, weight[c + 1]).astype(BF16)


def outer_mix_body(n, depth, *refs):
    packs, folded, out = refs[:n], refs[n:-1], refs[-1]
    for rows, merged in aggregates(packs, folded, out.shape[0] // n, depth):
        out[rows] = merged


def outer_body(n, depth, *refs):
    firsts, seconds, (mixed, weight) = refs[:n], refs[n : 2 * n], refs[2 * n : 2 * n + 2]
    query, numer, denom, inner, out_weight, pair_out, *share = refs[2 * n + 2 :]
    tok = mixed.shape[0] // n
    step = min(n, 2)
    for r in range(0, n, step):
        rows = slice(r * tok, (r + step) * tok)
        spots = [piece for i in range(r, r + step) for piece in (firsts[i][depth:], seconds[i][...])]
        normed = normalize(mixed[rows] + jnp.concatenate(spots, axis=0).astype(F32))
        for c in range(2):
            pair_out[c, rows] = dot(normed, weight[c + 1]).astype(BF16)
    if share:
        finish_body(1, query, numer, denom, inner, pair_out, out_weight, share[0])


def absorb(query, pairs):
    tok, width = query.shape
    group = min(width, 128)
    per = group // HEAD_DIM
    lanes = lax.broadcasted_iota(jnp.int32, (1, group), 1) // HEAD_DIM
    numers, denoms = [], []
    for g in range(width // group):
        cut = slice(g * group, (g + 1) * group)
        block = query[:, cut]
        stack = jnp.concatenate([jnp.where(lanes == h, block, jnp.zeros_like(block)) for h in range(per)], axis=0)
        numer, denom = 0.0, 0.0
        for pair in pairs:
            expos = jnp.exp(dot(stack, pair[0, :, cut], NT))
            denom = denom + jnp.sum(expos, axis=-1, keepdims=True)
            numer = numer + dot(expos.astype(BF16), pair[1, :, cut])
        denom = jnp.broadcast_to(denom, numer.shape)
        top, low = numer[:tok], denom[:tok]
        for h in range(1, per):
            top = jnp.where(lanes == h, numer[h * tok : (h + 1) * tok], top)
            low = jnp.where(lanes == h, denom[h * tok : (h + 1) * tok], low)
        numers.append(top)
        denoms.append(low)
    return jnp.concatenate(numers, axis=1), jnp.concatenate(denoms, axis=1)


def begin_body(query, pair, numer, denom):
    for r in range(0, query.shape[0], 256):
        rows = slice(r, r + 256)
        numer[rows], denom[rows] = absorb(query[rows], [pair])


def finish_body(distance, query, numer, denom, inner, outer, out_weight, *refs):
    out = refs[-1]
    tok = out.shape[0]
    rows = slice(distance * tok, (distance + 1) * tok)
    top, low = absorb(query[rows], [inner, outer])
    context = ((numer[rows] + top) / (denom[rows] + low)).astype(BF16)
    update = dot(context, out_weight[...])
    for ref in refs[:-1]:
        update = update + ref[...]
    out[...] = update.astype(out.dtype)


def shards(pixels, embed_weight, variable_embed, agg_key, agg_value, position, qkv_weight, out_weight):
    n = lax.axis_size("var")
    n_vars, n_pix, band_tok = pixels.shape
    d = embed_weight.shape[2]
    tok = position.shape[0]
    width = qkv_weight.shape[2]
    n_heads = agg_key.shape[1]
    all_vars = n_vars * n
    rows = n_vars * n_pix
    depth = rows * band_tok // d
    sds = jax.ShapeDtypeStruct
    table = embed_weight.reshape(rows, d)
    pix = pixels.reshape(rows, band_tok)
    key_t = jnp.transpose(agg_key)
    weight = jnp.transpose(qkv_weight, (1, 0, 2))

    cut = (tok - depth) // 2
    half, shared, *placed = call(
        pack_body,
        [sds((size, d), BF16) for size in (rows // 2, depth + tok + n_vars, depth + cut, tok - cut)],
        (table, variable_embed, pix, position),
        "pack",
        [pltpu.HBM] * 4,
        [pltpu.VMEM((n_vars, d), BF16), pltpu.SemaphoreType.DMA((5 + 2 * (d // band_tok),))],
    )
    others = range(1, n)
    near = [shifted(half, "var", r) for r in others]
    first, second = (outward(x) for x in placed)
    packs = [shared] + [shifted(shared, "var", r) for r in others]

    moved = (table, variable_embed, key_t, agg_value, weight, out_weight)
    key_t, agg_value, weight, out_weight, *folded = call(
        functools.partial(stage_body, len(moved)),
        [sds(a.shape, a.dtype) for a in moved[2:]]
        + [sds((d, rows), BF16), sds((d, n_vars), BF16), sds((n_heads, rows), F32), sds((n_heads, n_vars), F32)],
        moved,
        "stage",
        [pltpu.HBM] * len(moved),
        [pltpu.VMEM((rows, d), BF16), pltpu.VMEM((n_vars, d), BF16), pltpu.SemaphoreType.DMA((len(moved),))],
    )
    *near, _ = lax.optimization_barrier((*near, folded[2]))
    far = [inward(x) for x in near]
    first, second, _ = lax.optimization_barrier((first, second, folded[0]))
    firsts = [first] + [shifted(first, "var", r) for r in others]
    seconds = [second] + [shifted(second, "var", r) for r in others]
    *folded, merged, query, pair = call(
        functools.partial(band_body, n, depth),
        [
            sds((d, rows * n), BF16),
            sds((d, all_vars), BF16),
            sds((n_heads, rows * n), F32),
            sds((n_heads, all_vars), F32),
            sds((tok, d), F32),
            sds((band_tok, width), BF16),
            sds((2, band_tok, width), BF16),
        ],
        (*packs, *near, *far, *folded, key_t, agg_value, weight),
        "front_band",
        scratch=[pltpu.VMEM((rows, d), BF16)],
    )
    inner = inward(pair)
    totals = call(begin_body, [sds((band_tok, width), F32)] * 2, (query, pair), "attend_band")
    *firsts, _ = lax.optimization_barrier((*firsts, totals[0]))
    (mixed,) = call(
        functools.partial(outer_mix_body, n, depth), [sds((band_tok, d), F32)], (*firsts, *folded), "mix_outer"
    )
    *seconds, mixed = lax.optimization_barrier((*seconds, mixed))
    outer_pair, *share = call(
        functools.partial(outer_body, n, depth),
        [sds((2, band_tok, width), BF16)] + [sds((tok, d), BF16)] * (n > 1),
        (*firsts, *seconds, mixed, weight, query, *totals, inner, out_weight),
        "front_outer",
    )
    attended = (query, *totals, inner, outer_pair, out_weight)
    for r in range(2, n):
        share += call(functools.partial(finish_body, r), [sds((tok, d), BF16)], attended, "attend_later")
    ending = [shifted(x, "var", n - r) for r, x in enumerate(share, 1)]
    (update,) = call(
        functools.partial(finish_body, 0), [sds((tok, d), F32)], (*attended, merged), "attend_own"
    )
    for x in ending:
        update = update + x.astype(F32)
    return update.astype(BF16)


def solution(mesh):
    in_specs = (
        P("var", None, "band"),
        P("var", None, None),
        P("var", None),
        P(),
        P(),
        P(("band", "var"), None),
        P(None, None, "var"),
        P("var", None),
    )
    out_specs = P(("band", "var"), None)
    return jax.shard_map(shards, mesh=mesh, in_specs=in_specs, out_specs=out_specs, check_vma=False)
```

```python
import functools

import jax
import jax.numpy as jnp
from jax import lax
from jax.experimental import pallas as pl
from jax.experimental.pallas import tpu as pltpu
from jax.sharding import PartitionSpec as P

HEAD_DIM = 64
EPSILON = 1e-05
F32 = jnp.float32
BF16 = jnp.bfloat16
NT = (((1,), (1,)), ((), ()))
NN = (((1,), (0,)), ((), ()))


def dot(a, b, dims=NN):
    return lax.dot_general(a, b, dims, preferred_element_type=F32)


def shifted(block, axis, distance):
    n = lax.axis_size(axis)
    return lax.ppermute(block, axis, [((i + distance) % n, i) for i in range(n)])


def inward(block):
    return lax.ppermute(block, "band", [(i ^ 1, i) for i in range(lax.axis_size("band"))])


def outward(block):
    n = lax.axis_size("band")
    return lax.ppermute(block, "band", [(i, (i + 1 if i % 2 else i - 1) % n) for i in range(n)])


COST = {"mix_outer": 20.0, "front_band": 0.3}


def call(body, outs, args, name, spaces=None, scratch=()):
    spaces = spaces or [pltpu.VMEM] * len(args)
    args = [pltpu.with_memory_space_constraint(a, s) if s == pltpu.HBM else a for a, s in zip(args, spaces)]
    return pl.pallas_call(
        body,
        out_shape=outs,
        in_specs=[pl.BlockSpec(memory_space=space) for space in spaces],
        out_specs=[pl.BlockSpec(memory_space=pltpu.VMEM) for _ in outs],
        scratch_shapes=scratch,
        compiler_params=pltpu.CompilerParams(vmem_limit_bytes=32 * 1024 * 1024),
        cost_estimate=pl.CostEstimate(flops=int(COST.get(name, 0.0) * 1e9), bytes_accessed=0, transcendentals=0),
        name=name,
    )(*args)


def fold(table, offsets, key_t, agg_value):
    values = jnp.transpose(dot(table, agg_value)).astype(BF16)
    offset_values = jnp.transpose(dot(offsets, agg_value)).astype(BF16)
    return values, offset_values, dot(key_t, table, NT), dot(key_t, offsets, NT)


def pack_body(table, offsets, pix, position, shared, first, second, offsets_in, sems):
    rows, band_tok = pix.shape
    tok, d = position.shape
    half = table.shape[0] // 2
    blocks = d // band_tok
    depth = rows // blocks
    cut = first.shape[0] - depth
    side = lax.rem(lax.axis_index("band"), 2)
    moves = [
        (offsets, offsets_in),
        (table.at[pl.ds(pl.multiple_of(side * half, half), half)], shared.at[pl.ds(depth, half)]),
        (position.at[pl.ds(0, cut)], first.at[pl.ds(depth, cut)]),
        (position.at[pl.ds(cut, tok - cut)], second),
    ]
    for k in range(blocks):
        lanes = pl.ds(k * band_tok, band_tok)
        moves.append((pix.at[pl.ds(k * depth, depth)], shared.at[pl.ds(0, depth), lanes]))
        moves.append((pix.at[pl.ds(k * depth, depth)], first.at[pl.ds(0, depth), lanes]))
    copies = [pltpu.make_async_copy(a, b, sems.at[i]) for i, (a, b) in enumerate(moves)]
    for copy in copies:
        copy.start()
    for copy in copies:
        copy.wait()
    shared[depth + half :] = offsets_in[...]


def stage_body(n_in, *refs):
    sources, (table, offsets), staged = refs[:n_in], refs[-3:-1], refs[n_in : 2 * n_in - 2]
    folded, sems = refs[2 * n_in - 2 : -3], refs[-1]
    targets = [table, offsets, *staged]
    copies = [pltpu.make_async_copy(a, b, sems.at[i]) for i, (a, b) in enumerate(zip(sources, targets))]
    for copy in copies:
        copy.start()
    for copy in copies[:4]:
        copy.wait()
    for out, part in zip(folded, fold(*(ref[...] for ref in targets[:4]))):
        out[...] = part
    for copy in copies[4:]:
        copy.wait()


def aggregate(pix, values, offset_values, keys, offset_keys):
    n_heads, n_rows = keys.shape
    n_vars = offset_keys.shape[1]
    n_pix = n_rows // n_vars
    tok = pix.shape[1]
    rows = lax.broadcasted_iota(jnp.int32, (n_vars * n_heads, n_rows), 0) // n_heads
    cols = lax.broadcasted_iota(jnp.int32, (n_vars * n_heads, n_rows), 1) // n_pix
    spread = jnp.where(rows == cols, jnp.concatenate([keys] * n_vars, axis=0), 0.0)
    high = spread.astype(BF16)
    low = (spread - high.astype(F32)).astype(BF16)
    rows = lax.broadcasted_iota(jnp.int32, (n_vars * n_heads, n_vars), 0) // n_heads
    cols = lax.broadcasted_iota(jnp.int32, (n_vars * n_heads, n_vars), 1)
    base = jnp.sum(
        jnp.where(rows == cols, jnp.concatenate([offset_keys] * n_vars, axis=0), 0.0), axis=1, keepdims=True
    )
    scores = dot(high, pix) + dot(low, pix) + base
    expos = jnp.exp(scores).reshape(n_vars, n_heads, tok)
    weights = (expos / jnp.sum(expos, axis=0, keepdims=True)).astype(BF16).astype(F32)
    points = pix.astype(F32).reshape(n_vars, n_pix, tok)
    merged = []
    for h in range(n_heads):
        head = weights[:, h, :]
        mixed = (head[:, None, :] * points).reshape(n_rows, tok).astype(BF16)
        own = slice(h * HEAD_DIM, (h + 1) * HEAD_DIM)
        merged.append(dot(values[own], mixed) + dot(offset_values[own], head.astype(BF16)))
    return jnp.transpose(jnp.concatenate(merged, axis=0))


def normalize(merged):
    centre = jnp.mean(merged, axis=-1, keepdims=True)
    centred = merged - centre
    spread = jnp.mean(jnp.square(centred), axis=-1, keepdims=True)
    return (centred * lax.rsqrt(spread + EPSILON)).astype(BF16)


def aggregates(packs, folded, tok, depth):
    n = len(packs)
    step = min(n, 2)
    for r in range(0, n, step):
        parts = []
        for ref in packs:
            for k in range(ref.shape[1] // (n * tok)):
                pieces = []
                for i in range(step):
                    start = k * n * tok + lax.rem(lax.axis_index("var") + r + i, n) * tok
                    pieces.append(ref[:depth, pl.ds(pl.multiple_of(start, tok), tok)])
                parts.append(jnp.concatenate(pieces, axis=1))
        pix = jnp.concatenate(parts, axis=0)
        yield slice(r * tok, (r + step) * tok), aggregate(pix, *(ref[...] for ref in folded))


def band_body(n, depth, *refs):
    packs, far, mine = refs[:n], refs[n : 2 * n - 1], refs[2 * n - 1 : 2 * n + 3]
    positions, (key_t, agg_value, weight) = refs[2 * n + 3 : 3 * n + 3], refs[3 * n + 3 : 3 * n + 6]
    *folded, merged_out, query_out, pair_out, table = refs[3 * n + 6 :]
    tok = merged_out.shape[0]
    half = table.shape[0] // 2
    side = lax.rem(lax.axis_index("band"), 2)
    parts = [tuple(ref[...] for ref in mine)]
    for pack, other in zip(packs[1:], far):
        table[pl.ds(pl.multiple_of(side * half, half), half)] = pack[depth : depth + half]
        table[pl.ds(pl.multiple_of((1 - side) * half, half), half)] = other[...]
        parts.append(fold(table[...], pack[depth + half :], key_t[...], agg_value[...]))
    for out, shares in zip(folded, zip(*parts)):
        out[...] = jnp.concatenate(shares, axis=1)
    for rows, merged in aggregates(packs, folded, tok, depth):
        spots = positions[rows.start // tok : rows.stop // tok]
        merged = merged + jnp.concatenate([ref[...] for ref in spots], axis=0).astype(F32)
        if rows.start == 0:
            merged_out[...] = merged[:tok]
        normed = normalize(merged)
        query_out[rows] = (dot(normed, weight[0]).astype(BF16) * HEAD_DIM ** (-0.5)).astype(BF16)
        for c in range(2):
            pair_out[c, rows] = dot(normed, weight[c + 1]).astype(BF16)


def outer_mix_body(n, depth, *refs):
    packs, folded, out = refs[:n], refs[n:-1], refs[-1]
    for rows, merged in aggregates(packs, folded, out.shape[0] // n, depth):
        out[rows] = merged


def outer_body(n, depth, *refs):
    firsts, seconds, (mixed, weight) = refs[:n], refs[n : 2 * n], refs[2 * n : 2 * n + 2]
    query, numer, denom, inner, out_weight, pair_out, *share = refs[2 * n + 2 :]
    tok = mixed.shape[0] // n
    step = min(n, 2)
    for r in range(0, n, step):
        rows = slice(r * tok, (r + step) * tok)
        spots = [piece for i in range(r, r + step) for piece in (firsts[i][depth:], seconds[i][...])]
        normed = normalize(mixed[rows] + jnp.concatenate(spots, axis=0).astype(F32))
        for c in range(2):
            pair_out[c, rows] = dot(normed, weight[c + 1]).astype(BF16)
    if share:
        finish_body(1, query, numer, denom, inner, pair_out, out_weight, share[0])


def absorb(query, pairs):
    tok, width = query.shape
    group = min(width, 128)
    per = group // HEAD_DIM
    lanes = lax.broadcasted_iota(jnp.int32, (1, group), 1) // HEAD_DIM
    numers, denoms = [], []
    for g in range(width // group):
        cut = slice(g * group, (g + 1) * group)
        block = query[:, cut]
        stack = jnp.concatenate([jnp.where(lanes == h, block, jnp.zeros_like(block)) for h in range(per)], axis=0)
        numer, denom = 0.0, 0.0
        for pair in pairs:
            expos = jnp.exp(dot(stack, pair[0, :, cut], NT))
            denom = denom + jnp.sum(expos, axis=-1, keepdims=True)
            numer = numer + dot(expos.astype(BF16), pair[1, :, cut])
        denom = jnp.broadcast_to(denom, numer.shape)
        top, low = numer[:tok], denom[:tok]
        for h in range(1, per):
            top = jnp.where(lanes == h, numer[h * tok : (h + 1) * tok], top)
            low = jnp.where(lanes == h, denom[h * tok : (h + 1) * tok], low)
        numers.append(top)
        denoms.append(low)
    return jnp.concatenate(numers, axis=1), jnp.concatenate(denoms, axis=1)


def begin_body(query, pair, numer, denom):
    for r in range(0, query.shape[0], 256):
        rows = slice(r, r + 256)
        numer[rows], denom[rows] = absorb(query[rows], [pair])


def finish_body(distance, query, numer, denom, inner, outer, out_weight, *refs):
    out = refs[-1]
    tok = out.shape[0]
    rows = slice(distance * tok, (distance + 1) * tok)
    top, low = absorb(query[rows], [inner, outer])
    context = ((numer[rows] + top) / (denom[rows] + low)).astype(BF16)
    update = dot(context, out_weight[...])
    for ref in refs[:-1]:
        update = update + ref[...]
    out[...] = update.astype(out.dtype)


def shards(pixels, embed_weight, variable_embed, agg_key, agg_value, position, qkv_weight, out_weight):
    n = lax.axis_size("var")
    n_vars, n_pix, band_tok = pixels.shape
    d = embed_weight.shape[2]
    tok = position.shape[0]
    width = qkv_weight.shape[2]
    n_heads = agg_key.shape[1]
    all_vars = n_vars * n
    rows = n_vars * n_pix
    depth = rows * band_tok // d
    sds = jax.ShapeDtypeStruct
    table = embed_weight.reshape(rows, d)
    pix = pixels.reshape(rows, band_tok)
    key_t = jnp.transpose(agg_key)
    weight = jnp.transpose(qkv_weight, (1, 0, 2))

    cut = (tok - depth) // 2
    shared, *placed = call(
        pack_body,
        [sds((size, d), BF16) for size in (depth + rows // 2 + n_vars, depth + cut, tok - cut)],
        (table, variable_embed, pix, position),
        "pack",
        [pltpu.HBM] * 4,
        [pltpu.VMEM((n_vars, d), BF16), pltpu.SemaphoreType.DMA((4 + 2 * (d // band_tok),))],
    )
    others = range(1, n)
    near = [shifted(shared, "var", r) for r in others]
    first, second = (outward(x) for x in placed)
    positions = [shifted(position, "var", r) for r in others]

    moved = (table, variable_embed, key_t, agg_value, weight, out_weight, position)
    key_t, agg_value, weight, out_weight, position, *folded = call(
        functools.partial(stage_body, len(moved)),
        [sds(a.shape, a.dtype) for a in moved[2:]]
        + [sds((d, rows), BF16), sds((d, n_vars), BF16), sds((n_heads, rows), F32), sds((n_heads, n_vars), F32)],
        moved,
        "stage",
        [pltpu.HBM] * len(moved),
        [pltpu.VMEM((rows, d), BF16), pltpu.VMEM((n_vars, d), BF16), pltpu.SemaphoreType.DMA((len(moved),))],
    )
    near, positions, _ = lax.optimization_barrier((near, positions, folded[2]))
    packs = [shared] + near
    far = [inward(x[depth : depth + rows // 2]) for x in near]
    first, _ = lax.optimization_barrier((first, folded[0]))
    second, _ = lax.optimization_barrier((second, folded[1]))
    firsts = [first] + [shifted(first, "var", r) for r in others]
    seconds = [second] + [shifted(second, "var", r) for r in others]
    *folded, merged, query, pair = call(
        functools.partial(band_body, n, depth),
        [
            sds((d, rows * n), BF16),
            sds((d, all_vars), BF16),
            sds((n_heads, rows * n), F32),
            sds((n_heads, all_vars), F32),
            sds((tok, d), F32),
            sds((band_tok, width), BF16),
            sds((2, band_tok, width), BF16),
        ],
        (*packs, *far, *folded, position, *positions, key_t, agg_value, weight),
        "front_band",
        scratch=[pltpu.VMEM((rows, d), BF16)],
    )
    inner = inward(pair)
    totals = call(begin_body, [sds((band_tok, width), F32)] * 2, (query, pair), "attend_band")
    *firsts, _ = lax.optimization_barrier((*firsts, totals[0]))
    (mixed,) = call(
        functools.partial(outer_mix_body, n, depth), [sds((band_tok, d), F32)], (*firsts, *folded), "mix_outer"
    )
    *seconds, mixed = lax.optimization_barrier((*seconds, mixed))
    outer_pair, *share = call(
        functools.partial(outer_body, n, depth),
        [sds((2, band_tok, width), BF16)] + [sds((tok, d), BF16)] * (n > 1),
        (*firsts, *seconds, mixed, weight, query, *totals, inner, out_weight),
        "front_outer",
    )
    attended = (query, *totals, inner, outer_pair, out_weight)
    for r in range(2, n):
        share += call(functools.partial(finish_body, r), [sds((tok, d), BF16)], attended, "attend_later")
    ending = [shifted(x, "var", n - r) for r, x in enumerate(share, 1)]
    (update,) = call(
        functools.partial(finish_body, 0), [sds((tok, d), F32)], (*attended, merged), "attend_own"
    )
    for x in ending:
        update = update + x.astype(F32)
    return update.astype(BF16)


def solution(mesh):
    in_specs = (
        P("var", None, "band"),
        P("var", None, None),
        P("var", None),
        P(),
        P(),
        P(("band", "var"), None),
        P(None, None, "var"),
        P("var", None),
    )
    out_specs = P(("band", "var"), None)
    return jax.shard_map(shards, mesh=mesh, in_specs=in_specs, out_specs=out_specs, check_vma=False)
```

```python
import functools

import jax
import jax.numpy as jnp
from jax import lax
from jax.experimental import pallas as pl
from jax.experimental.pallas import tpu as pltpu
from jax.sharding import PartitionSpec as P

HEAD_DIM = 64
EPSILON = 1e-05
F32 = jnp.float32
BF16 = jnp.bfloat16
NT = (((1,), (1,)), ((), ()))
NN = (((1,), (0,)), ((), ()))


def dot(a, b, dims=NN):
    return lax.dot_general(a, b, dims, preferred_element_type=F32)


def shifted(block, axis, distance):
    n = lax.axis_size(axis)
    return lax.ppermute(block, axis, [((i + distance) % n, i) for i in range(n)])


def inward(block):
    return lax.ppermute(block, "band", [(i ^ 1, i) for i in range(lax.axis_size("band"))])


def outward(block):
    n = lax.axis_size("band")
    return lax.ppermute(block, "band", [(i, (i + 1 if i % 2 else i - 1) % n) for i in range(n)])


COST = {"mix_outer": 20.0, "front_band": 0.3}


def call(body, outs, args, name, spaces=None, scratch=()):
    spaces = spaces or [pltpu.VMEM] * len(args)
    args = [pltpu.with_memory_space_constraint(a, s) if s == pltpu.HBM else a for a, s in zip(args, spaces)]
    return pl.pallas_call(
        body,
        out_shape=outs,
        in_specs=[pl.BlockSpec(memory_space=space) for space in spaces],
        out_specs=[pl.BlockSpec(memory_space=pltpu.VMEM) for _ in outs],
        scratch_shapes=scratch,
        compiler_params=pltpu.CompilerParams(vmem_limit_bytes=32 * 1024 * 1024),
        cost_estimate=pl.CostEstimate(flops=int(COST.get(name, 0.0) * 1e9), bytes_accessed=0, transcendentals=0),
        name=name,
    )(*args)


def fold(table, offsets, key_t, agg_value):
    n_vars, n_heads = offsets.shape[0], key_t.shape[0]
    both = dot(jnp.concatenate([table, offsets], axis=0), agg_value)
    values = jnp.transpose(both[: table.shape[0]]).astype(BF16)
    spread = jnp.broadcast_to(both[table.shape[0] :][:, None, :], (n_vars, n_heads, both.shape[1]))
    heads = lax.broadcasted_iota(jnp.int32, spread.shape, 1)
    owners = lax.broadcasted_iota(jnp.int32, spread.shape, 2) // HEAD_DIM
    offset_values = jnp.where(heads == owners, spread, 0.0).reshape(n_vars * n_heads, -1).astype(BF16)
    return values, offset_values, dot(key_t, table, NT), dot(key_t, offsets, NT)


def pack_body(table, offsets, pix, position, shared, first, second, offsets_in, sems):
    rows, band_tok = pix.shape
    tok, d = position.shape
    half = table.shape[0] // 2
    blocks = d // band_tok
    depth = rows // blocks
    cut = first.shape[0] - depth
    side = lax.rem(lax.axis_index("band"), 2)
    moves = [
        (offsets, offsets_in),
        (table.at[pl.ds(pl.multiple_of(side * half, half), half)], shared.at[pl.ds(depth, half)]),
        (position.at[pl.ds(0, cut)], first.at[pl.ds(depth, cut)]),
        (position.at[pl.ds(cut, tok - cut)], second),
    ]
    for k in range(blocks):
        lanes = pl.ds(k * band_tok, band_tok)
        moves.append((pix.at[pl.ds(k * depth, depth)], shared.at[pl.ds(0, depth), lanes]))
        moves.append((pix.at[pl.ds(k * depth, depth)], first.at[pl.ds(0, depth), lanes]))
    copies = [pltpu.make_async_copy(a, b, sems.at[i]) for i, (a, b) in enumerate(moves)]
    for copy in copies:
        copy.start()
    for copy in copies:
        copy.wait()
    shared[depth + half :] = offsets_in[...]


def stage_body(n_in, *refs):
    sources, (table, offsets), staged = refs[:n_in], refs[-3:-1], refs[n_in : 2 * n_in - 2]
    folded, sems = refs[2 * n_in - 2 : -3], refs[-1]
    targets = [table, offsets, *staged]
    copies = [pltpu.make_async_copy(a, b, sems.at[i]) for i, (a, b) in enumerate(zip(sources, targets))]
    for copy in copies:
        copy.start()
    for copy in copies[:4]:
        copy.wait()
    for out, part in zip(folded, fold(*(ref[...] for ref in targets[:4]))):
        out[...] = part
    for copy in copies[4:]:
        copy.wait()


def aggregate(pix, values, offset_values, keys, offset_keys):
    n_heads, n_rows = keys.shape
    n_vars = offset_keys.shape[1]
    n_pix = n_rows // n_vars
    tok = pix.shape[1]
    rows = lax.broadcasted_iota(jnp.int32, (n_vars * n_heads, n_rows), 0) // n_heads
    cols = lax.broadcasted_iota(jnp.int32, (n_vars * n_heads, n_rows), 1) // n_pix
    spread = jnp.where(rows == cols, jnp.concatenate([keys] * n_vars, axis=0), 0.0)
    high = spread.astype(BF16)
    low = (spread - high.astype(F32)).astype(BF16)
    rows = lax.broadcasted_iota(jnp.int32, (n_vars * n_heads, n_vars), 0) // n_heads
    cols = lax.broadcasted_iota(jnp.int32, (n_vars * n_heads, n_vars), 1)
    base = jnp.sum(
        jnp.where(rows == cols, jnp.concatenate([offset_keys] * n_vars, axis=0), 0.0), axis=1, keepdims=True
    )
    scores = dot(high, pix) + dot(low, pix) + base
    expos = jnp.exp(scores).reshape(n_vars, n_heads, tok)
    weights = (expos / jnp.sum(expos, axis=0, keepdims=True)).astype(BF16)
    points = pix.reshape(n_vars, n_pix, tok)
    merged = []
    for h in range(n_heads):
        head = weights[:, h, :]
        mixed = (head[:, None, :] * points).reshape(n_rows, tok)
        own = slice(h * HEAD_DIM, (h + 1) * HEAD_DIM)
        merged.append(dot(values[own], mixed))
    shifts = dot(jnp.transpose(weights.reshape(n_vars * n_heads, tok)), offset_values)
    return jnp.transpose(jnp.concatenate(merged, axis=0)) + shifts


def normalize(merged):
    centre = jnp.mean(merged, axis=-1, keepdims=True)
    centred = merged - centre
    spread = jnp.mean(jnp.square(centred), axis=-1, keepdims=True)
    return (centred * lax.rsqrt(spread + EPSILON)).astype(BF16)


def aggregates(packs, folded, tok, depth):
    n = len(packs)
    step = min(n, 2)
    for r in range(0, n, step):
        parts = []
        for ref in packs:
            for k in range(ref.shape[1] // (n * tok)):
                pieces = []
                for i in range(step):
                    start = k * n * tok + lax.rem(lax.axis_index("var") + r + i, n) * tok
                    pieces.append(ref[:depth, pl.ds(pl.multiple_of(start, tok), tok)])
                parts.append(jnp.concatenate(pieces, axis=1))
        pix = jnp.concatenate(parts, axis=0)
        yield slice(r * tok, (r + step) * tok), aggregate(pix, *(ref[...] for ref in folded))


def band_body(n, depth, *refs):
    packs, far, mine = refs[:n], refs[n : 2 * n - 1], refs[2 * n - 1 : 2 * n + 3]
    positions, (key_t, agg_value, weight) = refs[2 * n + 3 : 3 * n + 3], refs[3 * n + 3 : 3 * n + 6]
    *folded, merged_out, query_out, pair_out, table = refs[3 * n + 6 :]
    tok = merged_out.shape[0]
    half = table.shape[0] // 2
    side = lax.rem(lax.axis_index("band"), 2)
    parts = [tuple(ref[...] for ref in mine)]
    for pack, other in zip(packs[1:], far):
        table[pl.ds(pl.multiple_of(side * half, half), half)] = pack[depth : depth + half]
        table[pl.ds(pl.multiple_of((1 - side) * half, half), half)] = other[...]
        parts.append(fold(table[...], pack[depth + half :], key_t[...], agg_value[...]))
    for out, shares in zip(folded, zip(*parts)):
        out[...] = jnp.concatenate(shares, axis=0 if out is folded[1] else 1)
    for rows, merged in aggregates(packs, folded, tok, depth):
        spots = positions[rows.start // tok : rows.stop // tok]
        merged = merged + jnp.concatenate([ref[...] for ref in spots], axis=0).astype(F32)
        if rows.start == 0:
            merged_out[...] = merged[:tok]
        normed = normalize(merged)
        query_out[rows] = (dot(normed, weight[0]).astype(BF16) * HEAD_DIM ** (-0.5)).astype(BF16)
        for c in range(2):
            pair_out[c, rows] = dot(normed, weight[c + 1]).astype(BF16)


def outer_mix_body(n, depth, *refs):
    packs, folded, out = refs[:n], refs[n:-1], refs[-1]
    for rows, merged in aggregates(packs, folded, out.shape[0] // n, depth):
        out[rows] = merged


def outer_body(n, depth, *refs):
    firsts, seconds, (mixed, weight) = refs[:n], refs[n : 2 * n], refs[2 * n : 2 * n + 2]
    query, numer, denom, inner, out_weight, pair_out, *share = refs[2 * n + 2 :]
    tok = mixed.shape[0] // n
    step = min(n, 2)
    for r in range(0, n, step):
        rows = slice(r * tok, (r + step) * tok)
        spots = [piece for i in range(r, r + step) for piece in (firsts[i][depth:], seconds[i][...])]
        normed = normalize(mixed[rows] + jnp.concatenate(spots, axis=0).astype(F32))
        for c in range(2):
            pair_out[c, rows] = dot(normed, weight[c + 1]).astype(BF16)
    if share:
        finish_body(1, query, numer, denom, inner, pair_out, out_weight, share[0])


def absorb(query, pairs):
    tok, width = query.shape
    group = min(width, 128)
    per = group // HEAD_DIM
    lanes = lax.broadcasted_iota(jnp.int32, (1, group), 1) // HEAD_DIM
    numers, denoms = [], []
    for g in range(width // group):
        cut = slice(g * group, (g + 1) * group)
        block = query[:, cut]
        stack = jnp.concatenate([jnp.where(lanes == h, block, jnp.zeros_like(block)) for h in range(per)], axis=0)
        numer, denom = 0.0, 0.0
        for pair in pairs:
            expos = jnp.exp(dot(stack, pair[0, :, cut], NT)).astype(BF16)
            values = jnp.concatenate([pair[1, :, cut], jnp.ones((pair.shape[1], group), BF16)], axis=1)
            both = dot(expos, values)
            numer = numer + both[:, :group]
            denom = denom + both[:, group:]
        top, low = numer[:tok], denom[:tok]
        for h in range(1, per):
            top = jnp.where(lanes == h, numer[h * tok : (h + 1) * tok], top)
            low = jnp.where(lanes == h, denom[h * tok : (h + 1) * tok], low)
        numers.append(top)
        denoms.append(low)
    return jnp.concatenate(numers, axis=1), jnp.concatenate(denoms, axis=1)


def begin_body(query, pair, numer, denom):
    for r in range(0, query.shape[0], 256):
        rows = slice(r, r + 256)
        numer[rows], denom[rows] = absorb(query[rows], [pair])


def finish_body(distance, query, numer, denom, inner, outer, out_weight, *refs):
    out = refs[-1]
    tok = out.shape[0]
    rows = slice(distance * tok, (distance + 1) * tok)
    top, low = absorb(query[rows], [inner, outer])
    context = ((numer[rows] + top) / (denom[rows] + low)).astype(BF16)
    update = dot(context, out_weight[...])
    for ref in refs[:-1]:
        update = update + ref[...]
    out[...] = update.astype(out.dtype)


def shards(pixels, embed_weight, variable_embed, agg_key, agg_value, position, qkv_weight, out_weight):
    n = lax.axis_size("var")
    n_vars, n_pix, band_tok = pixels.shape
    d = embed_weight.shape[2]
    tok = position.shape[0]
    width = qkv_weight.shape[2]
    n_heads = agg_key.shape[1]
    all_vars = n_vars * n
    rows = n_vars * n_pix
    depth = rows * band_tok // d
    sds = jax.ShapeDtypeStruct
    table = embed_weight.reshape(rows, d)
    pix = pixels.reshape(rows, band_tok)
    key_t = jnp.transpose(agg_key)
    weight = jnp.transpose(qkv_weight, (1, 0, 2))

    cut = (tok - depth) // 2
    shared, *placed = call(
        pack_body,
        [sds((size, d), BF16) for size in (depth + rows // 2 + n_vars, depth + cut, tok - cut)],
        (table, variable_embed, pix, position),
        "pack",
        [pltpu.HBM] * 4,
        [pltpu.VMEM((n_vars, d), BF16), pltpu.SemaphoreType.DMA((4 + 2 * (d // band_tok),))],
    )
    others = range(1, n)
    near = [shifted(shared, "var", r) for r in others]
    first, second = (outward(x) for x in placed)
    positions = [shifted(position, "var", r) for r in others]

    moved = (table, variable_embed, key_t, agg_value, weight, out_weight, position)
    key_t, agg_value, weight, out_weight, position, *folded = call(
        functools.partial(stage_body, len(moved)),
        [sds(a.shape, a.dtype) for a in moved[2:]]
        + [sds((d, rows), BF16), sds((n_vars * n_heads, d), BF16), sds((n_heads, rows), F32), sds((n_heads, n_vars), F32)],
        moved,
        "stage",
        [pltpu.HBM] * len(moved),
        [pltpu.VMEM((rows, d), BF16), pltpu.VMEM((n_vars, d), BF16), pltpu.SemaphoreType.DMA((len(moved),))],
    )
    near, positions, _ = lax.optimization_barrier((near, positions, folded[2]))
    packs = [shared] + near
    far = [inward(x[depth : depth + rows // 2]) for x in near]
    first, _ = lax.optimization_barrier((first, folded[0]))
    second, _ = lax.optimization_barrier((second, folded[1]))
    firsts = [first] + [shifted(first, "var", r) for r in others]
    seconds = [second] + [shifted(second, "var", r) for r in others]
    *folded, merged, query, pair = call(
        functools.partial(band_body, n, depth),
        [
            sds((d, rows * n), BF16),
            sds((all_vars * n_heads, d), BF16),
            sds((n_heads, rows * n), F32),
            sds((n_heads, all_vars), F32),
            sds((tok, d), F32),
            sds((band_tok, width), BF16),
            sds((2, band_tok, width), BF16),
        ],
        (*packs, *far, *folded, position, *positions, key_t, agg_value, weight),
        "front_band",
        scratch=[pltpu.VMEM((rows, d), BF16)],
    )
    inner = inward(pair)
    totals = call(begin_body, [sds((band_tok, width), F32)] * 2, (query, pair), "attend_band")
    *firsts, _ = lax.optimization_barrier((*firsts, totals[0]))
    (mixed,) = call(
        functools.partial(outer_mix_body, n, depth), [sds((band_tok, d), F32)], (*firsts, *folded), "mix_outer"
    )
    *seconds, mixed = lax.optimization_barrier((*seconds, mixed))
    outer_pair, *share = call(
        functools.partial(outer_body, n, depth),
        [sds((2, band_tok, width), BF16)] + [sds((tok, d), BF16)] * (n > 1),
        (*firsts, *seconds, mixed, weight, query, *totals, inner, out_weight),
        "front_outer",
    )
    attended = (query, *totals, inner, outer_pair, out_weight)
    for r in range(2, n):
        share += call(functools.partial(finish_body, r), [sds((tok, d), BF16)], attended, "attend_later")
    ending = [shifted(x, "var", n - r) for r, x in enumerate(share, 1)]
    (update,) = call(
        functools.partial(finish_body, 0), [sds((tok, d), F32)], (*attended, merged), "attend_own"
    )
    for x in ending:
        update = update + x.astype(F32)
    return update.astype(BF16)


def solution(mesh):
    in_specs = (
        P("var", None, "band"),
        P("var", None, None),
        P("var", None),
        P(),
        P(),
        P(("band", "var"), None),
        P(None, None, "var"),
        P("var", None),
    )
    out_specs = P(("band", "var"), None)
    return jax.shard_map(shards, mesh=mesh, in_specs=in_specs, out_specs=out_specs, check_vma=False)
```

```python
import functools

import jax
import jax.numpy as jnp
from jax import lax
from jax.experimental import pallas as pl
from jax.experimental.pallas import tpu as pltpu
from jax.sharding import PartitionSpec as P

HEAD_DIM = 64
EPSILON = 1e-05
F32 = jnp.float32
BF16 = jnp.bfloat16
NT = (((1,), (1,)), ((), ()))
NN = (((1,), (0,)), ((), ()))


def dot(a, b, dims=NN):
    return lax.dot_general(a, b, dims, preferred_element_type=F32)


def shifted(block, axis, distance):
    n = lax.axis_size(axis)
    return lax.ppermute(block, axis, [((i + distance) % n, i) for i in range(n)])


def inward(block):
    return lax.ppermute(block, "band", [(i ^ 1, i) for i in range(lax.axis_size("band"))])


def outward(block):
    n = lax.axis_size("band")
    return lax.ppermute(block, "band", [(i, (i + 1 if i % 2 else i - 1) % n) for i in range(n)])


COST = {"mix_outer": 20.0, "front_band": 0.3}


def call(body, outs, args, name, spaces=None, scratch=()):
    spaces = spaces or [pltpu.VMEM] * len(args)
    args = [pltpu.with_memory_space_constraint(a, s) if s == pltpu.HBM else a for a, s in zip(args, spaces)]
    return pl.pallas_call(
        body,
        out_shape=outs,
        in_specs=[pl.BlockSpec(memory_space=space) for space in spaces],
        out_specs=[pl.BlockSpec(memory_space=pltpu.VMEM) for _ in outs],
        scratch_shapes=scratch,
        compiler_params=pltpu.CompilerParams(vmem_limit_bytes=32 * 1024 * 1024),
        cost_estimate=pl.CostEstimate(flops=int(COST.get(name, 0.0) * 1e9), bytes_accessed=0, transcendentals=0),
        name=name,
    )(*args)


def fold(table, offsets, key_t, agg_value):
    n_vars, n_heads = offsets.shape[0], key_t.shape[0]
    both = dot(jnp.concatenate([table, offsets], axis=0), agg_value)
    values = jnp.transpose(both[: table.shape[0]]).astype(BF16)
    spread = jnp.broadcast_to(both[table.shape[0] :][:, None, :], (n_vars, n_heads, both.shape[1]))
    heads = lax.broadcasted_iota(jnp.int32, spread.shape, 1)
    owners = lax.broadcasted_iota(jnp.int32, spread.shape, 2) // HEAD_DIM
    offset_values = jnp.where(heads == owners, spread, 0.0).reshape(n_vars * n_heads, -1).astype(BF16)
    return values, offset_values, dot(key_t, table, NT), dot(key_t, offsets, NT)


def pack_body(table, offsets, pix, position, shared, first, second, offsets_in, sems):
    rows, band_tok = pix.shape
    tok, d = position.shape
    half = table.shape[0] // 2
    blocks = d // band_tok
    depth = rows // blocks
    cut = first.shape[0] - depth
    side = lax.rem(lax.axis_index("band"), 2)
    moves = [
        (offsets, offsets_in),
        (table.at[pl.ds(pl.multiple_of(side * half, half), half)], shared.at[pl.ds(depth, half)]),
        (position.at[pl.ds(0, cut)], first.at[pl.ds(depth, cut)]),
        (position.at[pl.ds(cut, tok - cut)], second),
    ]
    for k in range(blocks):
        lanes = pl.ds(k * band_tok, band_tok)
        moves.append((pix.at[pl.ds(k * depth, depth)], shared.at[pl.ds(0, depth), lanes]))
        moves.append((pix.at[pl.ds(k * depth, depth)], first.at[pl.ds(0, depth), lanes]))
    copies = [pltpu.make_async_copy(a, b, sems.at[i]) for i, (a, b) in enumerate(moves)]
    for copy in copies:
        copy.start()
    for copy in copies:
        copy.wait()
    shared[depth + half :] = offsets_in[...]


def stage_body(n_in, *refs):
    sources, (table, offsets), staged = refs[:n_in], refs[-3:-1], refs[n_in : 2 * n_in - 2]
    folded, sems = refs[2 * n_in - 2 : -3], refs[-1]
    targets = [table, offsets, *staged]
    copies = [pltpu.make_async_copy(a, b, sems.at[i]) for i, (a, b) in enumerate(zip(sources, targets))]
    for copy in copies:
        copy.start()
    for copy in copies[:4]:
        copy.wait()
    for out, part in zip(folded, fold(*(ref[...] for ref in targets[:4]))):
        out[...] = part
    for copy in copies[4:]:
        copy.wait()


def aggregate(pix, values, offset_values, keys, offset_keys):
    n_heads, n_rows = keys.shape
    n_vars = offset_keys.shape[1]
    n_pix = n_rows // n_vars
    tok = pix.shape[1]
    rows = lax.broadcasted_iota(jnp.int32, (n_vars * n_heads, n_rows), 0) // n_heads
    cols = lax.broadcasted_iota(jnp.int32, (n_vars * n_heads, n_rows), 1) // n_pix
    spread = jnp.where(rows == cols, jnp.concatenate([keys] * n_vars, axis=0), 0.0)
    high = spread.astype(BF16)
    low = (spread - high.astype(F32)).astype(BF16)
    rows = lax.broadcasted_iota(jnp.int32, (n_vars * n_heads, n_vars), 0) // n_heads
    cols = lax.broadcasted_iota(jnp.int32, (n_vars * n_heads, n_vars), 1)
    base = jnp.sum(
        jnp.where(rows == cols, jnp.concatenate([offset_keys] * n_vars, axis=0), 0.0), axis=1, keepdims=True
    )
    scores = dot(high, pix) + dot(low, pix) + base
    expos = jnp.exp(scores).reshape(n_vars, n_heads, tok)
    weights = (expos / jnp.sum(expos, axis=0, keepdims=True)).astype(BF16)
    points = pix.reshape(n_vars, n_pix, tok)
    merged = []
    for h in range(n_heads):
        head = weights[:, h, :]
        mixed = (head[:, None, :] * points).reshape(n_rows, tok)
        own = slice(h * HEAD_DIM, (h + 1) * HEAD_DIM)
        merged.append(dot(values[own], mixed))
    shifts = dot(jnp.transpose(weights.reshape(n_vars * n_heads, tok)), offset_values)
    return jnp.transpose(jnp.concatenate(merged, axis=0)) + shifts


def normalize(merged):
    centre = jnp.mean(merged, axis=-1, keepdims=True)
    centred = merged - centre
    spread = jnp.mean(jnp.square(centred), axis=-1, keepdims=True)
    return (centred * lax.rsqrt(spread + EPSILON)).astype(BF16)


def aggregates(packs, folded, tok, depth):
    n = len(packs)
    step = min(n, 2)
    for r in range(0, n, step):
        parts = []
        for ref in packs:
            for k in range(ref.shape[1] // (n * tok)):
                pieces = []
                for i in range(step):
                    start = k * n * tok + lax.rem(lax.axis_index("var") + r + i, n) * tok
                    pieces.append(ref[:depth, pl.ds(pl.multiple_of(start, tok), tok)])
                parts.append(jnp.concatenate(pieces, axis=1))
        pix = jnp.concatenate(parts, axis=0)
        yield slice(r * tok, (r + step) * tok), aggregate(pix, *(ref[...] for ref in folded))


def band_body(n, depth, *refs):
    packs, far, mine = refs[:n], refs[n : 2 * n - 1], refs[2 * n - 1 : 2 * n + 3]
    positions, (key_t, agg_value, weight) = refs[2 * n + 3 : 3 * n + 3], refs[3 * n + 3 : 3 * n + 6]
    *folded, merged_out, query_out, pair_out, table = refs[3 * n + 6 :]
    tok = merged_out.shape[0]
    half = table.shape[0] // 2
    side = lax.rem(lax.axis_index("band"), 2)
    parts = [tuple(ref[...] for ref in mine)]
    for pack, other in zip(packs[1:], far):
        table[pl.ds(pl.multiple_of(side * half, half), half)] = pack[depth : depth + half]
        table[pl.ds(pl.multiple_of((1 - side) * half, half), half)] = other[...]
        parts.append(fold(table[...], pack[depth + half :], key_t[...], agg_value[...]))
    for out, shares in zip(folded, zip(*parts)):
        out[...] = jnp.concatenate(shares, axis=0 if out is folded[1] else 1)
    for rows, merged in aggregates(packs, folded, tok, depth):
        spots = positions[rows.start // tok : rows.stop // tok]
        merged = merged + jnp.concatenate([ref[...] for ref in spots], axis=0).astype(F32)
        if rows.start == 0:
            merged_out[...] = merged[:tok]
        normed = normalize(merged)
        query_out[rows] = (dot(normed, weight[0]).astype(BF16) * HEAD_DIM ** (-0.5)).astype(BF16)
        for c in range(2):
            pair_out[c, rows] = dot(normed, weight[c + 1]).astype(BF16)


def outer_mix_body(n, depth, *refs):
    packs, folded, out = refs[:n], refs[n:-1], refs[-1]
    for rows, merged in aggregates(packs, folded, out.shape[0] // n, depth):
        out[rows] = merged


def outer_body(n, depth, *refs):
    firsts, seconds, (mixed, weight) = refs[:n], refs[n : 2 * n], refs[2 * n : 2 * n + 2]
    query, numer, denom, inner, out_weight, pair_out, *share = refs[2 * n + 2 :]
    tok = mixed.shape[0] // n
    step = min(n, 2)
    for r in range(0, n, step):
        rows = slice(r * tok, (r + step) * tok)
        spots = [piece for i in range(r, r + step) for piece in (firsts[i][depth:], seconds[i][...])]
        normed = normalize(mixed[rows] + jnp.concatenate(spots, axis=0).astype(F32))
        for c in range(2):
            pair_out[c, rows] = dot(normed, weight[c + 1]).astype(BF16)
    if share:
        finish_body(tok, query, numer, denom, inner, pair_out, out_weight, share[0])


def absorb(query, pairs):
    tok, width = query.shape
    group = min(width, 128)
    per = group // HEAD_DIM
    lanes = lax.broadcasted_iota(jnp.int32, (1, group), 1) // HEAD_DIM
    numers, denoms = [], []
    for g in range(width // group):
        cut = slice(g * group, (g + 1) * group)
        block = query[:, cut]
        stack = jnp.concatenate([jnp.where(lanes == h, block, jnp.zeros_like(block)) for h in range(per)], axis=0)
        numer, denom = 0.0, 0.0
        for pair in pairs:
            expos = jnp.exp(dot(stack, pair[0, :, cut], NT)).astype(BF16)
            values = jnp.concatenate([pair[1, :, cut], jnp.ones((pair.shape[1], group), BF16)], axis=1)
            both = dot(expos, values)
            numer = numer + both[:, :group]
            denom = denom + both[:, group:]
        top, low = numer[:tok], denom[:tok]
        for h in range(1, per):
            top = jnp.where(lanes == h, numer[h * tok : (h + 1) * tok], top)
            low = jnp.where(lanes == h, denom[h * tok : (h + 1) * tok], low)
        numers.append(top)
        denoms.append(low)
    return jnp.concatenate(numers, axis=1), jnp.concatenate(denoms, axis=1)


def begin_body(query, pair, numer, denom):
    for r in range(0, query.shape[0], 256):
        rows = slice(r, r + 256)
        numer[rows], denom[rows] = absorb(query[rows], [pair])


def finish_body(first, query, numer, denom, inner, outer, out_weight, *refs):
    out = refs[-1]
    rows = slice(first, first + out.shape[0])
    top, low = absorb(query[rows], [inner, outer])
    context = ((numer[rows] + top) / (denom[rows] + low)).astype(BF16)
    update = dot(context, out_weight[...])
    for ref in refs[:-1]:
        update = update + ref[...]
    out[...] = update.astype(out.dtype)


def shards(pixels, embed_weight, variable_embed, agg_key, agg_value, position, qkv_weight, out_weight):
    n = lax.axis_size("var")
    n_vars, n_pix, band_tok = pixels.shape
    d = embed_weight.shape[2]
    tok = position.shape[0]
    width = qkv_weight.shape[2]
    n_heads = agg_key.shape[1]
    all_vars = n_vars * n
    rows = n_vars * n_pix
    depth = rows * band_tok // d
    sds = jax.ShapeDtypeStruct
    table = embed_weight.reshape(rows, d)
    pix = pixels.reshape(rows, band_tok)
    key_t = jnp.transpose(agg_key)
    weight = jnp.transpose(qkv_weight, (1, 0, 2))

    cut = (tok - depth) // 2
    shared, *placed = call(
        pack_body,
        [sds((size, d), BF16) for size in (depth + rows // 2 + n_vars, depth + cut, tok - cut)],
        (table, variable_embed, pix, position),
        "pack",
        [pltpu.HBM] * 4,
        [pltpu.VMEM((n_vars, d), BF16), pltpu.SemaphoreType.DMA((4 + 2 * (d // band_tok),))],
    )
    others = range(1, n)
    near = [shifted(shared, "var", r) for r in others]
    first, second = (outward(x) for x in placed)
    positions = [shifted(position, "var", r) for r in others]

    moved = (table, variable_embed, key_t, agg_value, weight, out_weight, position)
    key_t, agg_value, weight, out_weight, position, *folded = call(
        functools.partial(stage_body, len(moved)),
        [sds(a.shape, a.dtype) for a in moved[2:]]
        + [sds((d, rows), BF16), sds((n_vars * n_heads, d), BF16), sds((n_heads, rows), F32), sds((n_heads, n_vars), F32)],
        moved,
        "stage",
        [pltpu.HBM] * len(moved),
        [pltpu.VMEM((rows, d), BF16), pltpu.VMEM((n_vars, d), BF16), pltpu.SemaphoreType.DMA((len(moved),))],
    )
    near, positions, _ = lax.optimization_barrier((near, positions, folded[2]))
    packs = [shared] + near
    far = [inward(x[depth : depth + rows // 2]) for x in near]
    first, _ = lax.optimization_barrier((first, folded[0]))
    second, _ = lax.optimization_barrier((second, folded[1]))
    firsts = [first] + [shifted(first, "var", r) for r in others]
    seconds = [second] + [shifted(second, "var", r) for r in others]
    *folded, merged, query, pair = call(
        functools.partial(band_body, n, depth),
        [
            sds((d, rows * n), BF16),
            sds((all_vars * n_heads, d), BF16),
            sds((n_heads, rows * n), F32),
            sds((n_heads, all_vars), F32),
            sds((tok, d), F32),
            sds((band_tok, width), BF16),
            sds((2, band_tok, width), BF16),
        ],
        (*packs, *far, *folded, position, *positions, key_t, agg_value, weight),
        "front_band",
        scratch=[pltpu.VMEM((rows, d), BF16)],
    )
    inner = inward(pair)
    totals = call(begin_body, [sds((band_tok, width), F32)] * 2, (query, pair), "attend_band")
    *firsts, _ = lax.optimization_barrier((*firsts, totals[0]))
    (mixed,) = call(
        functools.partial(outer_mix_body, n, depth), [sds((band_tok, d), F32)], (*firsts, *folded), "mix_outer"
    )
    *seconds, mixed = lax.optimization_barrier((*seconds, mixed))
    spans = [(0, tok * 5 // 8), (tok * 5 // 8, tok)]
    outer_pair, *share = call(
        functools.partial(outer_body, n, depth),
        [sds((2, band_tok, width), BF16)] + [sds((spans[0][1], d), BF16)] * (n > 1),
        (*firsts, *seconds, mixed, weight, query, *totals, inner, out_weight),
        "front_outer",
    )
    attended = (query, *totals, inner, outer_pair, out_weight)
    pieces = [[None] * len(spans) for _ in others]
    for r in others:
        for i, (start, stop) in enumerate(spans):
            if r > 1 or i > 0:
                share = call(
                    functools.partial(finish_body, r * tok + start), [sds((stop - start, d), BF16)], attended, "attend_later"
                )
            pieces[r - 1][i] = shifted(share[0], "var", n - r)
    (update,) = call(functools.partial(finish_body, 0), [sds((tok, d), F32)], (*attended, merged), "attend_own")
    for parts in pieces:
        update = update + jnp.concatenate(parts, axis=0).astype(F32)
    return update.astype(BF16)


def solution(mesh):
    in_specs = (
        P("var", None, "band"),
        P("var", None, None),
        P("var", None),
        P(),
        P(),
        P(("band", "var"), None),
        P(None, None, "var"),
        P("var", None),
    )
    out_specs = P(("band", "var"), None)
    return jax.shard_map(shards, mesh=mesh, in_specs=in_specs, out_specs=out_specs, check_vma=False)
```

```python
import functools

import jax
import jax.numpy as jnp
from jax import lax
from jax.experimental import pallas as pl
from jax.experimental.pallas import tpu as pltpu
from jax.sharding import PartitionSpec as P

HEAD_DIM = 64
EPSILON = 1e-05
F32 = jnp.float32
BF16 = jnp.bfloat16
NT = (((1,), (1,)), ((), ()))
NN = (((1,), (0,)), ((), ()))


def dot(a, b, dims=NN):
    return lax.dot_general(a, b, dims, preferred_element_type=F32)


def shifted(block, axis, distance):
    n = lax.axis_size(axis)
    return lax.ppermute(block, axis, [((i + distance) % n, i) for i in range(n)])


def inward(block):
    return lax.ppermute(block, "band", [(i ^ 1, i) for i in range(lax.axis_size("band"))])


def outward(block):
    n = lax.axis_size("band")
    return lax.ppermute(block, "band", [(i, (i + 1 if i % 2 else i - 1) % n) for i in range(n)])


COST = {"gate": 20.0, "front_band": 0.3}


def call(body, outs, args, name, spaces=None, scratch=()):
    spaces = spaces or [pltpu.VMEM] * len(args)
    args = [pltpu.with_memory_space_constraint(a, s) if s == pltpu.HBM else a for a, s in zip(args, spaces)]
    return pl.pallas_call(
        body,
        out_shape=outs,
        in_specs=[pl.BlockSpec(memory_space=space) for space in spaces],
        out_specs=[pl.BlockSpec(memory_space=pltpu.VMEM) for _ in outs],
        scratch_shapes=scratch,
        compiler_params=pltpu.CompilerParams(vmem_limit_bytes=32 * 1024 * 1024),
        cost_estimate=pl.CostEstimate(flops=int(COST.get(name, 0.0) * 1e9), bytes_accessed=0, transcendentals=0),
        name=name,
    )(*args)


def fold(table, offsets, key_t, agg_value):
    n_vars, n_heads = offsets.shape[0], key_t.shape[0]
    both = dot(jnp.concatenate([table, offsets], axis=0), agg_value)
    values = jnp.transpose(both[: table.shape[0]]).astype(BF16)
    spread = jnp.broadcast_to(both[table.shape[0] :][:, None, :], (n_vars, n_heads, both.shape[1]))
    heads = lax.broadcasted_iota(jnp.int32, spread.shape, 1)
    owners = lax.broadcasted_iota(jnp.int32, spread.shape, 2) // HEAD_DIM
    offset_values = jnp.where(heads == owners, spread, 0.0).reshape(n_vars * n_heads, -1).astype(BF16)
    return values, offset_values, dot(key_t, table, NT), dot(key_t, offsets, NT)


def pack_body(table, offsets, pix, position, shared, placed, offsets_in, sems):
    rows, band_tok = pix.shape
    tok, d = position.shape
    half = table.shape[0] // 2
    blocks = d // band_tok
    depth = rows // blocks
    side = lax.rem(lax.axis_index("band"), 2)
    moves = [
        (offsets, offsets_in),
        (table.at[pl.ds(pl.multiple_of(side * half, half), half)], shared.at[pl.ds(depth, half)]),
        (position, placed.at[pl.ds(depth, tok)]),
    ]
    for k in range(blocks):
        lanes = pl.ds(k * band_tok, band_tok)
        moves.append((pix.at[pl.ds(k * depth, depth)], shared.at[pl.ds(0, depth), lanes]))
        moves.append((pix.at[pl.ds(k * depth, depth)], placed.at[pl.ds(0, depth), lanes]))
    copies = [pltpu.make_async_copy(a, b, sems.at[i]) for i, (a, b) in enumerate(moves)]
    for copy in copies:
        copy.start()
    for copy in copies:
        copy.wait()
    shared[depth + half :] = offsets_in[...]


def stage_body(n_in, *refs):
    sources, (table, offsets), staged = refs[:n_in], refs[-3:-1], refs[n_in : 2 * n_in - 2]
    folded, sems = refs[2 * n_in - 2 : -3], refs[-1]
    targets = [table, offsets, *staged]
    copies = [pltpu.make_async_copy(a, b, sems.at[i]) for i, (a, b) in enumerate(zip(sources, targets))]
    for copy in copies:
        copy.start()
    for copy in copies[:4]:
        copy.wait()
    for out, part in zip(folded, fold(*(ref[...] for ref in targets[:4]))):
        out[...] = part
    for copy in copies[4:]:
        copy.wait()


def aggregate(pix, values, offset_values, keys, offset_keys):
    n_heads, n_rows = keys.shape
    n_vars = offset_keys.shape[1]
    n_pix = n_rows // n_vars
    tok = pix.shape[1]
    rows = lax.broadcasted_iota(jnp.int32, (n_vars * n_heads, n_rows), 0) // n_heads
    cols = lax.broadcasted_iota(jnp.int32, (n_vars * n_heads, n_rows), 1) // n_pix
    spread = jnp.where(rows == cols, jnp.concatenate([keys] * n_vars, axis=0), 0.0)
    high = spread.astype(BF16)
    low = (spread - high.astype(F32)).astype(BF16)
    rows = lax.broadcasted_iota(jnp.int32, (n_vars * n_heads, n_vars), 0) // n_heads
    cols = lax.broadcasted_iota(jnp.int32, (n_vars * n_heads, n_vars), 1)
    base = jnp.sum(
        jnp.where(rows == cols, jnp.concatenate([offset_keys] * n_vars, axis=0), 0.0), axis=1, keepdims=True
    )
    scores = dot(high, pix) + dot(low, pix) + base
    expos = jnp.exp(scores).reshape(n_vars, n_heads, tok)
    weights = (expos / jnp.sum(expos, axis=0, keepdims=True)).astype(BF16)
    points = pix.reshape(n_vars, n_pix, tok)
    merged = []
    for h in range(n_heads):
        head = weights[:, h, :]
        mixed = (head[:, None, :] * points).reshape(n_rows, tok)
        own = slice(h * HEAD_DIM, (h + 1) * HEAD_DIM)
        merged.append(dot(values[own], mixed))
    shifts = dot(jnp.transpose(weights.reshape(n_vars * n_heads, tok)), offset_values)
    return jnp.transpose(jnp.concatenate(merged, axis=0)) + shifts


def normalize(merged):
    centre = jnp.mean(merged, axis=-1, keepdims=True)
    centred = merged - centre
    spread = jnp.mean(jnp.square(centred), axis=-1, keepdims=True)
    return (centred * lax.rsqrt(spread + EPSILON)).astype(BF16)


def aggregates(packs, folded, tok, depth):
    n = len(packs)
    step = min(n, 2)
    for r in range(0, n, step):
        parts = []
        for ref in packs:
            for k in range(ref.shape[1] // (n * tok)):
                pieces = []
                for i in range(step):
                    start = k * n * tok + lax.rem(lax.axis_index("var") + r + i, n) * tok
                    pieces.append(ref[:depth, pl.ds(pl.multiple_of(start, tok), tok)])
                parts.append(jnp.concatenate(pieces, axis=1))
        pix = jnp.concatenate(parts, axis=0)
        yield slice(r * tok, (r + step) * tok), aggregate(pix, *(ref[...] for ref in folded))


def band_body(n, depth, *refs):
    packs, far, mine = refs[:n], refs[n : 2 * n - 1], refs[2 * n - 1 : 2 * n + 3]
    positions, (key_t, agg_value, weight) = refs[2 * n + 3 : 3 * n + 3], refs[3 * n + 3 : 3 * n + 6]
    *folded, merged_out, query_out, pair_out, table = refs[3 * n + 6 :]
    tok = merged_out.shape[0]
    half = table.shape[0] // 2
    side = lax.rem(lax.axis_index("band"), 2)
    parts = [tuple(ref[...] for ref in mine)]
    for pack, other in zip(packs[1:], far):
        table[pl.ds(pl.multiple_of(side * half, half), half)] = pack[depth : depth + half]
        table[pl.ds(pl.multiple_of((1 - side) * half, half), half)] = other[...]
        parts.append(fold(table[...], pack[depth + half :], key_t[...], agg_value[...]))
    for out, shares in zip(folded, zip(*parts)):
        out[...] = jnp.concatenate(shares, axis=0 if out is folded[1] else 1)
    for rows, merged in aggregates(packs, folded, tok, depth):
        spots = positions[rows.start // tok : rows.stop // tok]
        merged = merged + jnp.concatenate([ref[...] for ref in spots], axis=0).astype(F32)
        if rows.start == 0:
            merged_out[...] = merged[:tok]
        normed = normalize(merged)
        query_out[rows] = (dot(normed, weight[0]).astype(BF16) * HEAD_DIM ** (-0.5)).astype(BF16)
        for c in range(2):
            pair_out[c, rows] = dot(normed, weight[c + 1]).astype(BF16)


def outer_mix_body(n, depth, *refs):
    packs, folded, out = refs[:n], refs[n:-1], refs[-1]
    for rows, merged in aggregates(packs, folded, out.shape[0] // n, depth):
        out[rows] = merged


def gate_body(*refs):
    refs[-1][...] = jnp.zeros(refs[-1].shape, F32)


def outer_body(n, *refs):
    spots, (mixed, weight) = refs[:n], refs[n : n + 2]
    query, numer, denom, inner, out_weight, _, pair_out, *share = refs[n + 2 :]
    tok = mixed.shape[0] // n
    step = min(n, 2)
    for r in range(0, n, step):
        rows = slice(r * tok, (r + step) * tok)
        position = jnp.concatenate([ref[...] for ref in spots[r : r + step]], axis=0)
        normed = normalize(mixed[rows] + position.astype(F32))
        for c in range(2):
            pair_out[c, rows] = dot(normed, weight[c + 1]).astype(BF16)
    if share:
        finish_body(tok, query, numer, denom, inner, pair_out, out_weight, share[0])


def absorb(query, pairs):
    tok, width = query.shape
    group = min(width, 128)
    per = group // HEAD_DIM
    lanes = lax.broadcasted_iota(jnp.int32, (1, group), 1) // HEAD_DIM
    numers, denoms = [], []
    for g in range(width // group):
        cut = slice(g * group, (g + 1) * group)
        block = query[:, cut]
        stack = jnp.concatenate([jnp.where(lanes == h, block, jnp.zeros_like(block)) for h in range(per)], axis=0)
        numer, denom = 0.0, 0.0
        for pair in pairs:
            expos = jnp.exp(dot(stack, pair[0, :, cut], NT)).astype(BF16)
            values = jnp.concatenate([pair[1, :, cut], jnp.ones((pair.shape[1], group), BF16)], axis=1)
            both = dot(expos, values)
            numer = numer + both[:, :group]
            denom = denom + both[:, group:]
        top, low = numer[:tok], denom[:tok]
        for h in range(1, per):
            top = jnp.where(lanes == h, numer[h * tok : (h + 1) * tok], top)
            low = jnp.where(lanes == h, denom[h * tok : (h + 1) * tok], low)
        numers.append(top)
        denoms.append(low)
    return jnp.concatenate(numers, axis=1), jnp.concatenate(denoms, axis=1)


def begin_body(query, pair, numer, denom):
    for r in range(0, query.shape[0], 256):
        rows = slice(r, r + 256)
        numer[rows], denom[rows] = absorb(query[rows], [pair])


def finish_body(first, query, numer, denom, inner, outer, out_weight, *refs):
    out = refs[-1]
    rows = slice(first, first + out.shape[0])
    top, low = absorb(query[rows], [inner, outer])
    context = ((numer[rows] + top) / (denom[rows] + low)).astype(BF16)
    update = dot(context, out_weight[...])
    for ref in refs[:-1]:
        update = update + ref[...]
    out[...] = update.astype(out.dtype)


def shards(pixels, embed_weight, variable_embed, agg_key, agg_value, position, qkv_weight, out_weight):
    n = lax.axis_size("var")
    n_vars, n_pix, band_tok = pixels.shape
    d = embed_weight.shape[2]
    tok = position.shape[0]
    width = qkv_weight.shape[2]
    n_heads = agg_key.shape[1]
    all_vars = n_vars * n
    rows = n_vars * n_pix
    depth = rows * band_tok // d
    sds = jax.ShapeDtypeStruct
    table = embed_weight.reshape(rows, d)
    pix = pixels.reshape(rows, band_tok)
    key_t = jnp.transpose(agg_key)
    weight = jnp.transpose(qkv_weight, (1, 0, 2))

    shared, placed = call(
        pack_body,
        [sds((size, d), BF16) for size in (depth + rows // 2 + n_vars, depth + tok)],
        (table, variable_embed, pix, position),
        "pack",
        [pltpu.HBM] * 4,
        [pltpu.VMEM((n_vars, d), BF16), pltpu.SemaphoreType.DMA((3 + 2 * (d // band_tok),))],
    )
    others = range(1, n)
    near = [shifted(shared, "var", r) for r in others]
    outer = outward(placed)
    positions = [shifted(position, "var", r) for r in others]

    moved = (table, variable_embed, key_t, agg_value, weight, out_weight, position)
    key_t, agg_value, weight, out_weight, position, *folded = call(
        functools.partial(stage_body, len(moved)),
        [sds(a.shape, a.dtype) for a in moved[2:]]
        + [sds((d, rows), BF16), sds((n_vars * n_heads, d), BF16), sds((n_heads, rows), F32), sds((n_heads, n_vars), F32)],
        moved,
        "stage",
        [pltpu.HBM] * len(moved),
        [pltpu.VMEM((rows, d), BF16), pltpu.VMEM((n_vars, d), BF16), pltpu.SemaphoreType.DMA((len(moved),))],
    )
    near, _ = lax.optimization_barrier((near, folded[2]))
    packs = [shared] + near
    far = [inward(x[depth : depth + rows // 2]) for x in near]
    outer, _ = lax.optimization_barrier((outer, folded[0]))
    positions, _ = lax.optimization_barrier((positions, folded[1]))
    outer_pixs = [outer[:depth]] + [shifted(outer[:depth], "var", r) for r in others]
    outer_positions = [outer[depth:]] + [outward(x) for x in positions]
    *folded, merged, query, pair = call(
        functools.partial(band_body, n, depth),
        [
            sds((d, rows * n), BF16),
            sds((all_vars * n_heads, d), BF16),
            sds((n_heads, rows * n), F32),
            sds((n_heads, all_vars), F32),
            sds((tok, d), F32),
            sds((band_tok, width), BF16),
            sds((2, band_tok, width), BF16),
        ],
        (*packs, *far, *folded, position, *positions, key_t, agg_value, weight),
        "front_band",
        scratch=[pltpu.VMEM((rows, d), BF16)],
    )
    inner = inward(pair)
    totals = call(begin_body, [sds((band_tok, width), F32)] * 2, (query, pair), "attend_band")
    *outer_pixs, _ = lax.optimization_barrier((*outer_pixs, totals[0]))
    (mixed,) = call(
        functools.partial(outer_mix_body, n, depth), [sds((band_tok, d), F32)], (*outer_pixs, *folded), "mix_outer"
    )
    (ready,) = call(gate_body, [sds((8, 128), F32)], (mixed, *outer_positions[1:]), "gate")
    spans = [(0, tok * 5 // 8), (tok * 5 // 8, tok)]
    outer_pair, *share = call(
        functools.partial(outer_body, n),
        [sds((2, band_tok, width), BF16)] + [sds((spans[0][1], d), BF16)] * (n > 1),
        (*outer_positions, mixed, weight, query, *totals, inner, out_weight, ready),
        "front_outer",
    )
    attended = (query, *totals, inner, outer_pair, out_weight)
    pieces = [[None] * len(spans) for _ in others]
    for r in others:
        for i, (start, stop) in enumerate(spans):
            if r > 1 or i > 0:
                share = call(
                    functools.partial(finish_body, r * tok + start), [sds((stop - start, d), BF16)], attended, "attend_later"
                )
            pieces[r - 1][i] = shifted(share[0], "var", n - r)
    (update,) = call(functools.partial(finish_body, 0), [sds((tok, d), F32)], (*attended, merged), "attend_own")
    for parts in pieces:
        update = update + jnp.concatenate(parts, axis=0).astype(F32)
    return update.astype(BF16)


def solution(mesh):
    in_specs = (
        P("var", None, "band"),
        P("var", None, None),
        P("var", None),
        P(),
        P(),
        P(("band", "var"), None),
        P(None, None, "var"),
        P("var", None),
    )
    out_specs = P(("band", "var"), None)
    return jax.shard_map(shards, mesh=mesh, in_specs=in_specs, out_specs=out_specs, check_vma=False)
```

```python
import functools

import jax
import jax.numpy as jnp
from jax import lax
from jax.experimental import pallas as pl
from jax.experimental.pallas import tpu as pltpu
from jax.sharding import PartitionSpec as P

HEAD_DIM = 64
EPSILON = 1e-05
F32 = jnp.float32
BF16 = jnp.bfloat16
NT = (((1,), (1,)), ((), ()))
NN = (((1,), (0,)), ((), ()))


def dot(a, b, dims=NN):
    return lax.dot_general(a, b, dims, preferred_element_type=F32)


def shifted(block, axis, distance):
    n = lax.axis_size(axis)
    return lax.ppermute(block, axis, [((i + distance) % n, i) for i in range(n)])


def inward(block):
    return lax.ppermute(block, "band", [(i ^ 1, i) for i in range(lax.axis_size("band"))])


def outward(block):
    n = lax.axis_size("band")
    return lax.ppermute(block, "band", [(i, (i + 1 if i % 2 else i - 1) % n) for i in range(n)])


COST = {"gate": 20.0, "front_band": 0.3}


def call(body, outs, args, name, spaces=None, scratch=()):
    spaces = spaces or [pltpu.VMEM] * len(args)
    args = [pltpu.with_memory_space_constraint(a, s) if s == pltpu.HBM else a for a, s in zip(args, spaces)]
    return pl.pallas_call(
        body,
        out_shape=outs,
        in_specs=[pl.BlockSpec(memory_space=space) for space in spaces],
        out_specs=[pl.BlockSpec(memory_space=pltpu.VMEM) for _ in outs],
        scratch_shapes=scratch,
        compiler_params=pltpu.CompilerParams(vmem_limit_bytes=32 * 1024 * 1024),
        cost_estimate=pl.CostEstimate(flops=int(COST.get(name, 0.0) * 1e9), bytes_accessed=0, transcendentals=0),
        name=name,
    )(*args)


def fold(table, offsets, key_t, agg_value):
    n_vars, n_heads = offsets.shape[0], key_t.shape[0]
    both = dot(jnp.concatenate([table, offsets], axis=0), agg_value)
    values = jnp.transpose(both[: table.shape[0]]).astype(BF16)
    spread = jnp.broadcast_to(both[table.shape[0] :][:, None, :], (n_vars, n_heads, both.shape[1]))
    heads = lax.broadcasted_iota(jnp.int32, spread.shape, 1)
    owners = lax.broadcasted_iota(jnp.int32, spread.shape, 2) // HEAD_DIM
    offset_values = jnp.where(heads == owners, spread, 0.0).reshape(n_vars * n_heads, -1).astype(BF16)
    return values, offset_values, dot(key_t, table, NT), dot(key_t, offsets, NT)


def pack_body(table, offsets, pix, position, shared, placed, offsets_in, sems):
    rows, band_tok = pix.shape
    tok, d = position.shape
    half = table.shape[0] // 2
    blocks = d // band_tok
    depth = rows // blocks
    side = lax.rem(lax.axis_index("band"), 2)
    moves = [
        (offsets, offsets_in),
        (table.at[pl.ds(pl.multiple_of(side * half, half), half)], shared.at[pl.ds(depth, half)]),
        (position, placed.at[pl.ds(depth, tok)]),
    ]
    for k in range(blocks):
        lanes = pl.ds(k * band_tok, band_tok)
        moves.append((pix.at[pl.ds(k * depth, depth)], shared.at[pl.ds(0, depth), lanes]))
        moves.append((pix.at[pl.ds(k * depth, depth)], placed.at[pl.ds(0, depth), lanes]))
    copies = [pltpu.make_async_copy(a, b, sems.at[i]) for i, (a, b) in enumerate(moves)]
    for copy in copies:
        copy.start()
    for copy in copies:
        copy.wait()
    shared[depth + half :] = offsets_in[...]


def stage_body(n_in, *refs):
    sources, (table, offsets), staged = refs[:n_in], refs[-3:-1], refs[n_in : 2 * n_in - 2]
    folded, sems = refs[2 * n_in - 2 : -3], refs[-1]
    targets = [table, offsets, *staged]
    copies = [pltpu.make_async_copy(a, b, sems.at[i]) for i, (a, b) in enumerate(zip(sources, targets))]
    for copy in copies:
        copy.start()
    for copy in copies[:4]:
        copy.wait()
    for out, part in zip(folded, fold(*(ref[...] for ref in targets[:4]))):
        out[...] = part
    for copy in copies[4:]:
        copy.wait()


def aggregate(pix, values, offset_values, keys, offset_keys):
    n_heads, n_rows = keys.shape
    n_vars = offset_keys.shape[1]
    n_pix = n_rows // n_vars
    tok = pix.shape[1]
    rows = lax.broadcasted_iota(jnp.int32, (n_vars * n_heads, n_rows), 0) // n_heads
    cols = lax.broadcasted_iota(jnp.int32, (n_vars * n_heads, n_rows), 1) // n_pix
    spread = jnp.where(rows == cols, jnp.concatenate([keys] * n_vars, axis=0), 0.0)
    high = spread.astype(BF16)
    low = (spread - high.astype(F32)).astype(BF16)
    rows = lax.broadcasted_iota(jnp.int32, (n_vars * n_heads, n_vars), 0) // n_heads
    cols = lax.broadcasted_iota(jnp.int32, (n_vars * n_heads, n_vars), 1)
    base = jnp.sum(
        jnp.where(rows == cols, jnp.concatenate([offset_keys] * n_vars, axis=0), 0.0), axis=1, keepdims=True
    )
    scores = dot(high, pix) + dot(low, pix) + base
    expos = jnp.exp(scores).reshape(n_vars, n_heads, tok)
    weights = (expos / jnp.sum(expos, axis=0, keepdims=True)).astype(BF16)
    points = pix.reshape(n_vars, n_pix, tok)
    merged = []
    for h in range(n_heads):
        head = weights[:, h, :]
        mixed = (head[:, None, :] * points).reshape(n_rows, tok)
        own = slice(h * HEAD_DIM, (h + 1) * HEAD_DIM)
        merged.append(dot(values[own], mixed))
    shifts = dot(jnp.transpose(weights.reshape(n_vars * n_heads, tok)), offset_values)
    return jnp.transpose(jnp.concatenate(merged, axis=0)) + shifts


def normalize(merged):
    centre = jnp.mean(merged, axis=-1, keepdims=True)
    centred = merged - centre
    spread = jnp.mean(jnp.square(centred), axis=-1, keepdims=True)
    return (centred * lax.rsqrt(spread + EPSILON)).astype(BF16)


def aggregates(packs, folded, tok, depth):
    n = len(packs)
    step = min(n, 2)
    for r in range(0, n, step):
        parts = []
        for ref in packs:
            for k in range(ref.shape[1] // (n * tok)):
                pieces = []
                for i in range(step):
                    start = k * n * tok + lax.rem(lax.axis_index("var") + r + i, n) * tok
                    pieces.append(ref[:depth, pl.ds(pl.multiple_of(start, tok), tok)])
                parts.append(jnp.concatenate(pieces, axis=1))
        pix = jnp.concatenate(parts, axis=0)
        yield slice(r * tok, (r + step) * tok), aggregate(pix, *(ref[...] for ref in folded))


def band_body(n, depth, *refs):
    packs, far, mine = refs[:n], refs[n : 2 * n - 1], refs[2 * n - 1 : 2 * n + 3]
    positions, (key_t, agg_value, weight) = refs[2 * n + 3 : 3 * n + 3], refs[3 * n + 3 : 3 * n + 6]
    *folded, merged_out, query_out, pair_out, table = refs[3 * n + 6 :]
    tok = merged_out.shape[0]
    half = table.shape[0] // 2
    side = lax.rem(lax.axis_index("band"), 2)
    parts = [tuple(ref[...] for ref in mine)]
    for pack, other in zip(packs[1:], far):
        table[pl.ds(pl.multiple_of(side * half, half), half)] = pack[depth : depth + half]
        table[pl.ds(pl.multiple_of((1 - side) * half, half), half)] = other[...]
        parts.append(fold(table[...], pack[depth + half :], key_t[...], agg_value[...]))
    for out, shares in zip(folded, zip(*parts)):
        out[...] = jnp.concatenate(shares, axis=0 if out is folded[1] else 1)
    for rows, merged in aggregates(packs, folded, tok, depth):
        spots = positions[rows.start // tok : rows.stop // tok]
        merged = merged + jnp.concatenate([ref[...] for ref in spots], axis=0).astype(F32)
        if rows.start == 0:
            merged_out[...] = merged[:tok]
        normed = normalize(merged)
        query_out[rows] = (dot(normed, weight[0]).astype(BF16) * HEAD_DIM ** (-0.5)).astype(BF16)
        for c in range(2):
            pair_out[c, rows] = dot(normed, weight[c + 1]).astype(BF16)


def outer_mix_body(n, depth, *refs):
    packs, folded, out = refs[:n], refs[n:-1], refs[-1]
    for rows, merged in aggregates(packs, folded, out.shape[0] // n, depth):
        out[rows] = merged


def gate_body(*refs):
    refs[-1][...] = jnp.zeros(refs[-1].shape, F32)


def outer_body(n, depth, *refs):
    heads, tails, (mixed, weight) = refs[:n], refs[n : 2 * n], refs[2 * n : 2 * n + 2]
    query, numer, denom, inner, out_weight, _, pair_out, *share = refs[2 * n + 2 :]
    tok = mixed.shape[0] // n
    step = min(n, 2)
    for r in range(0, n, step):
        rows = slice(r * tok, (r + step) * tok)
        spots = [piece for i in range(r, r + step) for piece in (heads[i][depth:], tails[i][...])]
        position = jnp.concatenate(spots, axis=0)
        normed = normalize(mixed[rows] + position.astype(F32))
        for c in range(2):
            pair_out[c, rows] = dot(normed, weight[c + 1]).astype(BF16)
    if share:
        finish_body(tok, query, numer, denom, inner, pair_out, out_weight, share[0])


def absorb(query, pairs):
    tok, width = query.shape
    group = min(width, 128)
    per = group // HEAD_DIM
    lanes = lax.broadcasted_iota(jnp.int32, (1, group), 1) // HEAD_DIM
    numers, denoms = [], []
    for g in range(width // group):
        cut = slice(g * group, (g + 1) * group)
        block = query[:, cut]
        stack = jnp.concatenate([jnp.where(lanes == h, block, jnp.zeros_like(block)) for h in range(per)], axis=0)
        numer, denom = 0.0, 0.0
        for pair in pairs:
            expos = jnp.exp(dot(stack, pair[0, :, cut], NT)).astype(BF16)
            values = jnp.concatenate([pair[1, :, cut], jnp.ones((pair.shape[1], group), BF16)], axis=1)
            both = dot(expos, values)
            numer = numer + both[:, :group]
            denom = denom + both[:, group:]
        top, low = numer[:tok], denom[:tok]
        for h in range(1, per):
            top = jnp.where(lanes == h, numer[h * tok : (h + 1) * tok], top)
            low = jnp.where(lanes == h, denom[h * tok : (h + 1) * tok], low)
        numers.append(top)
        denoms.append(low)
    return jnp.concatenate(numers, axis=1), jnp.concatenate(denoms, axis=1)


def begin_body(query, pair, numer, denom):
    for r in range(0, query.shape[0], 256):
        rows = slice(r, r + 256)
        numer[rows], denom[rows] = absorb(query[rows], [pair])


def finish_body(first, query, numer, denom, inner, outer, out_weight, *refs):
    out = refs[-1]
    rows = slice(first, first + out.shape[0])
    top, low = absorb(query[rows], [inner, outer])
    context = ((numer[rows] + top) / (denom[rows] + low)).astype(BF16)
    update = dot(context, out_weight[...])
    for ref in refs[:-1]:
        update = update + ref[...]
    out[...] = update.astype(out.dtype)


def shards(pixels, embed_weight, variable_embed, agg_key, agg_value, position, qkv_weight, out_weight):
    n = lax.axis_size("var")
    n_vars, n_pix, band_tok = pixels.shape
    d = embed_weight.shape[2]
    tok = position.shape[0]
    width = qkv_weight.shape[2]
    n_heads = agg_key.shape[1]
    all_vars = n_vars * n
    rows = n_vars * n_pix
    depth = rows * band_tok // d
    sds = jax.ShapeDtypeStruct
    table = embed_weight.reshape(rows, d)
    pix = pixels.reshape(rows, band_tok)
    key_t = jnp.transpose(agg_key)
    weight = jnp.transpose(qkv_weight, (1, 0, 2))

    shared, placed = call(
        pack_body,
        [sds((size, d), BF16) for size in (depth + rows // 2 + n_vars, depth + tok)],
        (table, variable_embed, pix, position),
        "pack",
        [pltpu.HBM] * 4,
        [pltpu.VMEM((n_vars, d), BF16), pltpu.SemaphoreType.DMA((3 + 2 * (d // band_tok),))],
    )
    others = range(1, n)
    near = [shifted(shared, "var", r) for r in others]
    outer = outward(placed)
    positions = [shifted(position, "var", r) for r in others]

    moved = (table, variable_embed, key_t, agg_value, weight, out_weight, position)
    key_t, agg_value, weight, out_weight, position, *folded = call(
        functools.partial(stage_body, len(moved)),
        [sds(a.shape, a.dtype) for a in moved[2:]]
        + [sds((d, rows), BF16), sds((n_vars * n_heads, d), BF16), sds((n_heads, rows), F32), sds((n_heads, n_vars), F32)],
        moved,
        "stage",
        [pltpu.HBM] * len(moved),
        [pltpu.VMEM((rows, d), BF16), pltpu.VMEM((n_vars, d), BF16), pltpu.SemaphoreType.DMA((len(moved),))],
    )
    near, _ = lax.optimization_barrier((near, folded[2]))
    packs = [shared] + near
    far = [inward(x[depth : depth + rows // 2]) for x in near]
    outer, _ = lax.optimization_barrier((outer, folded[0]))
    positions, _ = lax.optimization_barrier((positions, folded[1]))
    lead = 16
    cut = depth + lead
    outer_heads = [outer[:cut]] + [shifted(outer[:cut], "var", r) for r in others]
    outer_tails = [outer[cut:]] + [outward(x[lead:]) for x in positions]
    *folded, merged, query, pair = call(
        functools.partial(band_body, n, depth),
        [
            sds((d, rows * n), BF16),
            sds((all_vars * n_heads, d), BF16),
            sds((n_heads, rows * n), F32),
            sds((n_heads, all_vars), F32),
            sds((tok, d), F32),
            sds((band_tok, width), BF16),
            sds((2, band_tok, width), BF16),
        ],
        (*packs, *far, *folded, position, *positions, key_t, agg_value, weight),
        "front_band",
        scratch=[pltpu.VMEM((rows, d), BF16)],
    )
    inner = inward(pair)
    totals = call(begin_body, [sds((band_tok, width), F32)] * 2, (query, pair), "attend_band")
    *outer_heads, _ = lax.optimization_barrier((*outer_heads, totals[0]))
    (mixed,) = call(
        functools.partial(outer_mix_body, n, depth), [sds((band_tok, d), F32)], (*outer_heads, *folded), "mix_outer"
    )
    (ready,) = call(gate_body, [sds((8, 128), F32)], (mixed, *outer_tails[1:]), "gate")
    spans = [(0, tok * 5 // 8), (tok * 5 // 8, tok)]
    outer_pair, *share = call(
        functools.partial(outer_body, n, depth),
        [sds((2, band_tok, width), BF16)] + [sds((spans[0][1], d), BF16)] * (n > 1),
        (*outer_heads, *outer_tails, mixed, weight, query, *totals, inner, out_weight, ready),
        "front_outer",
    )
    attended = (query, *totals, inner, outer_pair, out_weight)
    pieces = [[None] * len(spans) for _ in others]
    for r in others:
        for i, (start, stop) in enumerate(spans):
            if r > 1 or i > 0:
                share = call(
                    functools.partial(finish_body, r * tok + start), [sds((stop - start, d), BF16)], attended, "attend_later"
                )
            pieces[r - 1][i] = shifted(share[0], "var", n - r)
    (update,) = call(functools.partial(finish_body, 0), [sds((tok, d), F32)], (*attended, merged), "attend_own")
    for parts in pieces:
        update = update + jnp.concatenate(parts, axis=0).astype(F32)
    return update.astype(BF16)


def solution(mesh):
    in_specs = (
        P("var", None, "band"),
        P("var", None, None),
        P("var", None),
        P(),
        P(),
        P(("band", "var"), None),
        P(None, None, "var"),
        P("var", None),
    )
    out_specs = P(("band", "var"), None)
    return jax.shard_map(shards, mesh=mesh, in_specs=in_specs, out_specs=out_specs, check_vma=False)
```

```python
import functools

import jax
import jax.numpy as jnp
from jax import lax
from jax.experimental import pallas as pl
from jax.experimental.pallas import tpu as pltpu
from jax.sharding import PartitionSpec as P

HEAD_DIM = 64
EPSILON = 1e-05
F32 = jnp.float32
BF16 = jnp.bfloat16
NT = (((1,), (1,)), ((), ()))
NN = (((1,), (0,)), ((), ()))


def dot(a, b, dims=NN):
    return lax.dot_general(a, b, dims, preferred_element_type=F32)


def shifted(block, axis, distance):
    n = lax.axis_size(axis)
    return lax.ppermute(block, axis, [((i + distance) % n, i) for i in range(n)])


def inward(block):
    return lax.ppermute(block, "band", [(i ^ 1, i) for i in range(lax.axis_size("band"))])


def outward(block):
    n = lax.axis_size("band")
    return lax.ppermute(block, "band", [(i, (i + 1 if i % 2 else i - 1) % n) for i in range(n)])


COST = {"gate": 20.0, "front_band": 0.3}


def call(body, outs, args, name, spaces=None, scratch=()):
    spaces = spaces or [pltpu.VMEM] * len(args)
    args = [pltpu.with_memory_space_constraint(a, s) if s == pltpu.HBM else a for a, s in zip(args, spaces)]
    return pl.pallas_call(
        body,
        out_shape=outs,
        in_specs=[pl.BlockSpec(memory_space=space) for space in spaces],
        out_specs=[pl.BlockSpec(memory_space=pltpu.VMEM) for _ in outs],
        scratch_shapes=scratch,
        compiler_params=pltpu.CompilerParams(vmem_limit_bytes=32 * 1024 * 1024),
        cost_estimate=pl.CostEstimate(flops=int(COST.get(name, 0.0) * 1e9), bytes_accessed=0, transcendentals=0),
        name=name,
    )(*args)


def fold(table, offsets, key_t, agg_value):
    n_vars, n_heads = offsets.shape[0], key_t.shape[0]
    both = dot(jnp.concatenate([table, offsets], axis=0), agg_value)
    values = jnp.transpose(both[: table.shape[0]]).astype(BF16)
    spread = jnp.broadcast_to(both[table.shape[0] :][:, None, :], (n_vars, n_heads, both.shape[1]))
    heads = lax.broadcasted_iota(jnp.int32, spread.shape, 1)
    owners = lax.broadcasted_iota(jnp.int32, spread.shape, 2) // HEAD_DIM
    offset_values = jnp.where(heads == owners, spread, 0.0).reshape(n_vars * n_heads, -1).astype(BF16)
    return values, offset_values, dot(key_t, table, NT), dot(key_t, offsets, NT)


def pack_body(table, offsets, pix, position, shared, placed, offsets_in, sems):
    rows, band_tok = pix.shape
    tok, d = position.shape
    half = table.shape[0] // 2
    blocks = d // band_tok
    depth = rows // blocks
    side = lax.rem(lax.axis_index("band"), 2)
    moves = [
        (offsets, offsets_in),
        (table.at[pl.ds(pl.multiple_of(side * half, half), half)], shared.at[pl.ds(depth, half)]),
        (position, placed.at[pl.ds(depth, tok)]),
    ]
    for k in range(blocks):
        lanes = pl.ds(k * band_tok, band_tok)
        moves.append((pix.at[pl.ds(k * depth, depth)], shared.at[pl.ds(0, depth), lanes]))
        moves.append((pix.at[pl.ds(k * depth, depth)], placed.at[pl.ds(0, depth), lanes]))
    copies = [pltpu.make_async_copy(a, b, sems.at[i]) for i, (a, b) in enumerate(moves)]
    for copy in copies:
        copy.start()
    for copy in copies:
        copy.wait()
    shared[depth + half :] = offsets_in[...]


def stage_body(n_in, *refs):
    sources, (table, offsets), staged = refs[:n_in], refs[-3:-1], refs[n_in : 2 * n_in - 2]
    folded, sems = refs[2 * n_in - 2 : -3], refs[-1]
    targets = [table, offsets, *staged]
    copies = [pltpu.make_async_copy(a, b, sems.at[i]) for i, (a, b) in enumerate(zip(sources, targets))]
    for copy in copies:
        copy.start()
    for copy in copies[:4]:
        copy.wait()
    for out, part in zip(folded, fold(*(ref[...] for ref in targets[:4]))):
        out[...] = part
    for copy in copies[4:]:
        copy.wait()


def aggregate(pix, values, offset_values, keys, offset_keys):
    n_heads, n_rows = keys.shape
    n_vars = offset_keys.shape[1]
    n_pix = n_rows // n_vars
    tok = pix.shape[1]
    rows = lax.broadcasted_iota(jnp.int32, (n_vars * n_heads, n_rows), 0) // n_heads
    cols = lax.broadcasted_iota(jnp.int32, (n_vars * n_heads, n_rows), 1) // n_pix
    spread = jnp.where(rows == cols, jnp.concatenate([keys] * n_vars, axis=0), 0.0)
    high = spread.astype(BF16)
    low = (spread - high.astype(F32)).astype(BF16)
    rows = lax.broadcasted_iota(jnp.int32, (n_vars * n_heads, n_vars), 0) // n_heads
    cols = lax.broadcasted_iota(jnp.int32, (n_vars * n_heads, n_vars), 1)
    base = jnp.sum(
        jnp.where(rows == cols, jnp.concatenate([offset_keys] * n_vars, axis=0), 0.0), axis=1, keepdims=True
    )
    scores = dot(high, pix) + dot(low, pix) + base
    expos = jnp.exp(scores).reshape(n_vars, n_heads, tok)
    weights = (expos / jnp.sum(expos, axis=0, keepdims=True)).astype(BF16)
    points = pix.reshape(n_vars, n_pix, tok)
    merged = []
    for h in range(n_heads):
        head = weights[:, h, :]
        mixed = (head[:, None, :] * points).reshape(n_rows, tok)
        own = slice(h * HEAD_DIM, (h + 1) * HEAD_DIM)
        merged.append(dot(values[own], mixed))
    shifts = dot(jnp.transpose(weights.reshape(n_vars * n_heads, tok)), offset_values)
    return jnp.transpose(jnp.concatenate(merged, axis=0)) + shifts


def normalize(merged):
    centre = jnp.mean(merged, axis=-1, keepdims=True)
    centred = merged - centre
    spread = jnp.mean(jnp.square(centred), axis=-1, keepdims=True)
    return (centred * lax.rsqrt(spread + EPSILON)).astype(BF16)


def query_of(normed, weight):
    return (dot(normed, weight[0]).astype(BF16) * HEAD_DIM ** (-0.5)).astype(BF16)


def aggregates(packs, folded, tok, depth):
    n = len(packs)
    step = min(n, 2)
    for r in range(0, n, step):
        parts = []
        for ref in packs:
            for k in range(ref.shape[1] // (n * tok)):
                pieces = []
                for i in range(step):
                    start = k * n * tok + lax.rem(lax.axis_index("var") + r + i, n) * tok
                    pieces.append(ref[:depth, pl.ds(pl.multiple_of(start, tok), tok)])
                parts.append(jnp.concatenate(pieces, axis=1))
        pix = jnp.concatenate(parts, axis=0)
        yield slice(r * tok, (r + step) * tok), aggregate(pix, *(ref[...] for ref in folded))


def band_body(n, depth, *refs):
    packs, far, mine = refs[:n], refs[n : 2 * n - 1], refs[2 * n - 1 : 2 * n + 3]
    positions, (key_t, agg_value, weight) = refs[2 * n + 3 : 3 * n + 3], refs[3 * n + 3 : 3 * n + 6]
    *folded, merged_out, normed_out, query_out, pair_out, table = refs[3 * n + 6 :]
    tok = merged_out.shape[0]
    half = table.shape[0] // 2
    side = lax.rem(lax.axis_index("band"), 2)
    parts = [tuple(ref[...] for ref in mine)]
    for pack, other in zip(packs[1:], far):
        table[pl.ds(pl.multiple_of(side * half, half), half)] = pack[depth : depth + half]
        table[pl.ds(pl.multiple_of((1 - side) * half, half), half)] = other[...]
        parts.append(fold(table[...], pack[depth + half :], key_t[...], agg_value[...]))
    for out, shares in zip(folded, zip(*parts)):
        out[...] = jnp.concatenate(shares, axis=0 if out is folded[1] else 1)
    for rows, merged in aggregates(packs, folded, tok, depth):
        spots = positions[rows.start // tok : rows.stop // tok]
        merged = merged + jnp.concatenate([ref[...] for ref in spots], axis=0).astype(F32)
        normed = normalize(merged)
        rest = normed
        if rows.start == 0:
            merged_out[...] = merged[:tok]
            normed_out[...] = normed[:tok]
            rest = normed[tok:]
        if rest.shape[0] > 0:
            query_out[rows.stop - rest.shape[0] - tok : rows.stop - tok] = query_of(rest, weight)
        for c in range(2):
            pair_out[c, rows] = dot(normed, weight[c + 1]).astype(BF16)


def outer_mix_body(n, depth, *refs):
    packs, folded, out = refs[:n], refs[n:-1], refs[-1]
    for rows, merged in aggregates(packs, folded, out.shape[0] // n, depth):
        out[rows] = merged


def gate_body(*refs):
    refs[-1][...] = jnp.zeros(refs[-1].shape, F32)


def outer_body(n, depth, *refs):
    heads, tails, (mixed, weight) = refs[:n], refs[n : 2 * n], refs[2 * n : 2 * n + 2]
    query, numer, denom, inner, out_weight, _, pair_out, *share = refs[2 * n + 2 :]
    tok = mixed.shape[0] // n
    step = min(n, 2)
    for r in range(0, n, step):
        rows = slice(r * tok, (r + step) * tok)
        spots = [piece for i in range(r, r + step) for piece in (heads[i][depth:], tails[i][...])]
        position = jnp.concatenate(spots, axis=0)
        normed = normalize(mixed[rows] + position.astype(F32))
        for c in range(2):
            pair_out[c, rows] = dot(normed, weight[c + 1]).astype(BF16)
    if share:
        finish_body(0, query, numer, denom, inner, pair_out, out_weight, share[0])


def absorb(query, pairs):
    tok, width = query.shape
    group = min(width, 128)
    per = group // HEAD_DIM
    lanes = lax.broadcasted_iota(jnp.int32, (1, group), 1) // HEAD_DIM
    numers, denoms = [], []
    for g in range(width // group):
        cut = slice(g * group, (g + 1) * group)
        block = query[:, cut]
        stack = jnp.concatenate([jnp.where(lanes == h, block, jnp.zeros_like(block)) for h in range(per)], axis=0)
        numer, denom = 0.0, 0.0
        for pair in pairs:
            expos = jnp.exp(dot(stack, pair[0, :, cut], NT)).astype(BF16)
            values = jnp.concatenate([pair[1, :, cut], jnp.ones((pair.shape[1], group), BF16)], axis=1)
            both = dot(expos, values)
            numer = numer + both[:, :group]
            denom = denom + both[:, group:]
        top, low = numer[:tok], denom[:tok]
        for h in range(1, per):
            top = jnp.where(lanes == h, numer[h * tok : (h + 1) * tok], top)
            low = jnp.where(lanes == h, denom[h * tok : (h + 1) * tok], low)
        numers.append(top)
        denoms.append(low)
    return jnp.concatenate(numers, axis=1), jnp.concatenate(denoms, axis=1)


def begin_body(query, pair, numer, denom):
    for r in range(0, query.shape[0], 256):
        rows = slice(r, r + 256)
        numer[rows], denom[rows] = absorb(query[rows], [pair])


def finish_body(first, query, numer, denom, inner, outer, out_weight, out):
    rows = slice(first, first + out.shape[0])
    top, low = absorb(query[rows], [inner, outer])
    context = ((numer[rows] + top) / (denom[rows] + low)).astype(BF16)
    out[...] = dot(context, out_weight[...]).astype(out.dtype)


def own_body(normed, weight, pair, inner, outer, out_weight, merged, out):
    top, low = absorb(query_of(normed[...], weight), [pair, inner, outer])
    out[...] = merged[...] + dot((top / low).astype(BF16), out_weight[...])


def shards(pixels, embed_weight, variable_embed, agg_key, agg_value, position, qkv_weight, out_weight):
    n = lax.axis_size("var")
    n_vars, n_pix, band_tok = pixels.shape
    d = embed_weight.shape[2]
    tok = position.shape[0]
    width = qkv_weight.shape[2]
    n_heads = agg_key.shape[1]
    all_vars = n_vars * n
    rows = n_vars * n_pix
    depth = rows * band_tok // d
    sds = jax.ShapeDtypeStruct
    table = embed_weight.reshape(rows, d)
    pix = pixels.reshape(rows, band_tok)
    key_t = jnp.transpose(agg_key)
    weight = jnp.transpose(qkv_weight, (1, 0, 2))

    shared, placed = call(
        pack_body,
        [sds((size, d), BF16) for size in (depth + rows // 2 + n_vars, depth + tok)],
        (table, variable_embed, pix, position),
        "pack",
        [pltpu.HBM] * 4,
        [pltpu.VMEM((n_vars, d), BF16), pltpu.SemaphoreType.DMA((3 + 2 * (d // band_tok),))],
    )
    others = range(1, n)
    near = [shifted(shared, "var", r) for r in others]
    outer = outward(placed)
    positions = [shifted(position, "var", r) for r in others]

    moved = (table, variable_embed, key_t, agg_value, weight, out_weight, position)
    key_t, agg_value, weight, out_weight, position, *folded = call(
        functools.partial(stage_body, len(moved)),
        [sds(a.shape, a.dtype) for a in moved[2:]]
        + [sds((d, rows), BF16), sds((n_vars * n_heads, d), BF16), sds((n_heads, rows), F32), sds((n_heads, n_vars), F32)],
        moved,
        "stage",
        [pltpu.HBM] * len(moved),
        [pltpu.VMEM((rows, d), BF16), pltpu.VMEM((n_vars, d), BF16), pltpu.SemaphoreType.DMA((len(moved),))],
    )
    near, _ = lax.optimization_barrier((near, folded[2]))
    packs = [shared] + near
    far = [inward(x[depth : depth + rows // 2]) for x in near]
    outer, _ = lax.optimization_barrier((outer, folded[0]))
    positions, _ = lax.optimization_barrier((positions, folded[1]))
    lead = 16
    cut = depth + lead
    outer_heads = [outer[:cut]] + [shifted(outer[:cut], "var", r) for r in others]
    outer_tails = [outer[cut:]] + [outward(x[lead:]) for x in positions]
    *folded, merged, normed, query, pair = call(
        functools.partial(band_body, n, depth),
        [
            sds((d, rows * n), BF16),
            sds((all_vars * n_heads, d), BF16),
            sds((n_heads, rows * n), F32),
            sds((n_heads, all_vars), F32),
            sds((tok, d), F32),
            sds((tok, d), BF16),
            sds((band_tok - tok, width), BF16),
            sds((2, band_tok, width), BF16),
        ],
        (*packs, *far, *folded, position, *positions, key_t, agg_value, weight),
        "front_band",
        scratch=[pltpu.VMEM((rows, d), BF16)],
    )
    inner = inward(pair)
    totals = call(begin_body, [sds((band_tok - tok, width), F32)] * 2, (query, pair), "attend_band")
    *outer_heads, _ = lax.optimization_barrier((*outer_heads, totals[0]))
    (mixed,) = call(
        functools.partial(outer_mix_body, n, depth), [sds((band_tok, d), F32)], (*outer_heads, *folded), "mix_outer"
    )
    (ready,) = call(gate_body, [sds((8, 128), F32)], (mixed, *outer_tails[1:]), "gate")
    spans = [(0, tok * 5 // 8), (tok * 5 // 8, tok)]
    outer_pair, *share = call(
        functools.partial(outer_body, n, depth),
        [sds((2, band_tok, width), BF16)] + [sds((spans[0][1], d), BF16)] * (n > 1),
        (*outer_heads, *outer_tails, mixed, weight, query, *totals, inner, out_weight, ready),
        "front_outer",
    )
    attended = (query, *totals, inner, outer_pair, out_weight)
    pieces = [[None] * len(spans) for _ in others]
    for r in others:
        for i, (start, stop) in enumerate(spans):
            if r > 1 or i > 0:
                share = call(
                    functools.partial(finish_body, (r - 1) * tok + start), [sds((stop - start, d), BF16)], attended, "attend_later"
                )
            pieces[r - 1][i] = shifted(share[0], "var", n - r)
    (update,) = call(
        own_body, [sds((tok, d), F32)], (normed, weight, pair, inner, outer_pair, out_weight, merged), "attend_own"
    )
    for parts in pieces:
        update = update + jnp.concatenate(parts, axis=0).astype(F32)
    return update.astype(BF16)


def solution(mesh):
    in_specs = (
        P("var", None, "band"),
        P("var", None, None),
        P("var", None),
        P(),
        P(),
        P(("band", "var"), None),
        P(None, None, "var"),
        P("var", None),
    )
    out_specs = P(("band", "var"), None)
    return jax.shard_map(shards, mesh=mesh, in_specs=in_specs, out_specs=out_specs, check_vma=False)
```

```python
import functools

import jax
import jax.numpy as jnp
from jax import lax
from jax.experimental import pallas as pl
from jax.experimental.pallas import tpu as pltpu
from jax.sharding import PartitionSpec as P

HEAD_DIM = 64
EPSILON = 1e-05
F32 = jnp.float32
BF16 = jnp.bfloat16
NT = (((1,), (1,)), ((), ()))
NN = (((1,), (0,)), ((), ()))


def dot(a, b, dims=NN):
    return lax.dot_general(a, b, dims, preferred_element_type=F32)


def shifted(block, axis, distance):
    n = lax.axis_size(axis)
    return lax.ppermute(block, axis, [((i + distance) % n, i) for i in range(n)])


def inward(block):
    return lax.ppermute(block, "band", [(i ^ 1, i) for i in range(lax.axis_size("band"))])


def outward(block):
    n = lax.axis_size("band")
    return lax.ppermute(block, "band", [(i, (i + 1 if i % 2 else i - 1) % n) for i in range(n)])


COST = {"gate": 20.0, "front_band": 0.3}


def call(body, outs, args, name, spaces=None, scratch=()):
    spaces = spaces or [pltpu.VMEM] * len(args)
    args = [pltpu.with_memory_space_constraint(a, s) if s == pltpu.HBM else a for a, s in zip(args, spaces)]
    return pl.pallas_call(
        body,
        out_shape=outs,
        in_specs=[pl.BlockSpec(memory_space=space) for space in spaces],
        out_specs=[pl.BlockSpec(memory_space=pltpu.VMEM) for _ in outs],
        scratch_shapes=scratch,
        compiler_params=pltpu.CompilerParams(vmem_limit_bytes=32 * 1024 * 1024),
        cost_estimate=pl.CostEstimate(flops=int(COST.get(name, 0.0) * 1e9), bytes_accessed=0, transcendentals=0),
        name=name,
    )(*args)


def fold(table, offsets, key_t, agg_value):
    n_vars, n_heads = offsets.shape[0], key_t.shape[0]
    both = dot(jnp.concatenate([table, offsets], axis=0), agg_value)
    values = jnp.transpose(both[: table.shape[0]]).astype(BF16)
    spread = jnp.broadcast_to(both[table.shape[0] :][:, None, :], (n_vars, n_heads, both.shape[1]))
    heads = lax.broadcasted_iota(jnp.int32, spread.shape, 1)
    owners = lax.broadcasted_iota(jnp.int32, spread.shape, 2) // HEAD_DIM
    offset_values = jnp.where(heads == owners, spread, 0.0).reshape(n_vars * n_heads, -1).astype(BF16)
    return values, offset_values, dot(key_t, table, NT), dot(key_t, offsets, NT)


def pack_body(table, offsets, pix, position, shared, placed, offsets_in, sems):
    rows, band_tok = pix.shape
    tok, d = position.shape
    half = table.shape[0] // 2
    blocks = d // band_tok
    depth = rows // blocks
    side = lax.rem(lax.axis_index("band"), 2)
    moves = [
        (offsets, offsets_in),
        (table.at[pl.ds(pl.multiple_of(side * half, half), half)], shared.at[pl.ds(depth, half)]),
        (position, placed.at[pl.ds(depth, tok)]),
    ]
    for k in range(blocks):
        lanes = pl.ds(k * band_tok, band_tok)
        moves.append((pix.at[pl.ds(k * depth, depth)], shared.at[pl.ds(0, depth), lanes]))
        moves.append((pix.at[pl.ds(k * depth, depth)], placed.at[pl.ds(0, depth), lanes]))
    copies = [pltpu.make_async_copy(a, b, sems.at[i]) for i, (a, b) in enumerate(moves)]
    for copy in copies:
        copy.start()
    for copy in copies:
        copy.wait()
    shared[depth + half :] = offsets_in[...]


def stage_body(n_in, *refs):
    sources, (table, offsets), staged = refs[:n_in], refs[-3:-1], refs[n_in : 2 * n_in - 2]
    folded, sems = refs[2 * n_in - 2 : -3], refs[-1]
    targets = [table, offsets, *staged]
    copies = [pltpu.make_async_copy(a, b, sems.at[i]) for i, (a, b) in enumerate(zip(sources, targets))]
    for copy in copies:
        copy.start()
    for copy in copies[:4]:
        copy.wait()
    for out, part in zip(folded, fold(*(ref[...] for ref in targets[:4]))):
        out[...] = part
    for copy in copies[4:]:
        copy.wait()


def aggregate(pix, values, offset_values, keys, offset_keys):
    n_heads, n_rows = keys.shape
    n_vars = offset_keys.shape[1]
    n_pix = n_rows // n_vars
    tok = pix.shape[1]
    rows = lax.broadcasted_iota(jnp.int32, (n_vars * n_heads, n_rows), 0) // n_heads
    cols = lax.broadcasted_iota(jnp.int32, (n_vars * n_heads, n_rows), 1) // n_pix
    spread = jnp.where(rows == cols, jnp.concatenate([keys] * n_vars, axis=0), 0.0)
    high = spread.astype(BF16)
    low = (spread - high.astype(F32)).astype(BF16)
    rows = lax.broadcasted_iota(jnp.int32, (n_vars * n_heads, n_vars), 0) // n_heads
    cols = lax.broadcasted_iota(jnp.int32, (n_vars * n_heads, n_vars), 1)
    base = jnp.sum(
        jnp.where(rows == cols, jnp.concatenate([offset_keys] * n_vars, axis=0), 0.0), axis=1, keepdims=True
    )
    scores = dot(high, pix) + dot(low, pix) + base
    expos = jnp.exp(scores).reshape(n_vars, n_heads, tok)
    weights = (expos / jnp.sum(expos, axis=0, keepdims=True)).astype(BF16)
    points = pix.reshape(n_vars, n_pix, tok)
    merged = []
    for h in range(n_heads):
        head = weights[:, h, :]
        mixed = (head[:, None, :] * points).reshape(n_rows, tok)
        own = slice(h * HEAD_DIM, (h + 1) * HEAD_DIM)
        merged.append(dot(values[own], mixed))
    shifts = dot(jnp.transpose(weights.reshape(n_vars * n_heads, tok)), offset_values)
    return jnp.transpose(jnp.concatenate(merged, axis=0)) + shifts


def normalize(merged):
    centre = jnp.mean(merged, axis=-1, keepdims=True)
    centred = merged - centre
    spread = jnp.mean(jnp.square(centred), axis=-1, keepdims=True)
    return (centred * lax.rsqrt(spread + EPSILON)).astype(BF16)


def query_of(normed, weight):
    return (dot(normed, weight[0]).astype(BF16) * HEAD_DIM ** (-0.5)).astype(BF16)


def aggregates(packs, folded, tok, depth):
    n = len(packs)
    step = min(n, 2)
    for r in range(0, n, step):
        parts = []
        for ref in packs:
            for k in range(ref.shape[1] // (n * tok)):
                pieces = []
                for i in range(step):
                    start = k * n * tok + lax.rem(lax.axis_index("var") + r + i, n) * tok
                    pieces.append(ref[:depth, pl.ds(pl.multiple_of(start, tok), tok)])
                parts.append(jnp.concatenate(pieces, axis=1))
        pix = jnp.concatenate(parts, axis=0)
        yield slice(r * tok, (r + step) * tok), aggregate(pix, *(ref[...] for ref in folded))


def band_body(n, depth, *refs):
    packs, far, mine = refs[:n], refs[n : 2 * n - 1], refs[2 * n - 1 : 2 * n + 3]
    positions, (key_t, agg_value, weight) = refs[2 * n + 3 : 3 * n + 3], refs[3 * n + 3 : 3 * n + 6]
    *folded, merged_out, normed_out, query_out, pair_out, table = refs[3 * n + 6 :]
    tok = merged_out.shape[0]
    half = table.shape[0] // 2
    side = lax.rem(lax.axis_index("band"), 2)
    parts = [tuple(ref[...] for ref in mine)]
    for pack, other in zip(packs[1:], far):
        table[pl.ds(pl.multiple_of(side * half, half), half)] = pack[depth : depth + half]
        table[pl.ds(pl.multiple_of((1 - side) * half, half), half)] = other[...]
        parts.append(fold(table[...], pack[depth + half :], key_t[...], agg_value[...]))
    for out, shares in zip(folded, zip(*parts)):
        out[...] = jnp.concatenate(shares, axis=0 if out is folded[1] else 1)
    for rows, merged in aggregates(packs, folded, tok, depth):
        spots = positions[rows.start // tok : rows.stop // tok]
        merged = merged + jnp.concatenate([ref[ref.shape[0] - tok :] for ref in spots], axis=0).astype(F32)
        normed = normalize(merged)
        rest = normed
        if rows.start == 0:
            merged_out[...] = merged[:tok]
            normed_out[...] = normed[:tok]
            rest = normed[tok:]
        if rest.shape[0] > 0:
            query_out[rows.stop - rest.shape[0] - tok : rows.stop - tok] = query_of(rest, weight)
        for c in range(2):
            pair_out[c, rows] = dot(normed, weight[c + 1]).astype(BF16)


def outer_mix_body(n, depth, *refs):
    packs, folded, out = refs[:n], refs[n:-1], refs[-1]
    for rows, merged in aggregates(packs, folded, out.shape[0] // n, depth):
        out[rows] = merged


def gate_body(*refs):
    refs[-1][...] = jnp.zeros(refs[-1].shape, F32)


def outer_body(n, depth, *refs):
    heads, tails, (mixed, weight) = refs[:n], refs[n : 2 * n], refs[2 * n : 2 * n + 2]
    query, numer, denom, inner, out_weight, _, pair_out, *share = refs[2 * n + 2 :]
    tok = mixed.shape[0] // n
    step = min(n, 2)
    for r in range(0, n, step):
        rows = slice(r * tok, (r + step) * tok)
        spots = [piece for i in range(r, r + step) for piece in (heads[i][depth:], tails[i][...])]
        position = jnp.concatenate(spots, axis=0)
        normed = normalize(mixed[rows] + position.astype(F32))
        for c in range(2):
            pair_out[c, rows] = dot(normed, weight[c + 1]).astype(BF16)
    if share:
        finish_body(0, query, numer, denom, inner, pair_out, out_weight, share[0])


def absorb(query, pairs):
    tok, width = query.shape
    group = min(width, 128)
    per = group // HEAD_DIM
    lanes = lax.broadcasted_iota(jnp.int32, (1, group), 1) // HEAD_DIM
    numers, denoms = [], []
    for g in range(width // group):
        cut = slice(g * group, (g + 1) * group)
        block = query[:, cut]
        stack = jnp.concatenate([jnp.where(lanes == h, block, jnp.zeros_like(block)) for h in range(per)], axis=0)
        numer, denom = 0.0, 0.0
        for pair in pairs:
            expos = jnp.exp(dot(stack, pair[0, :, cut], NT)).astype(BF16)
            values = jnp.concatenate([pair[1, :, cut], jnp.ones((pair.shape[1], group), BF16)], axis=1)
            both = dot(expos, values)
            numer = numer + both[:, :group]
            denom = denom + both[:, group:]
        top, low = numer[:tok], denom[:tok]
        for h in range(1, per):
            top = jnp.where(lanes == h, numer[h * tok : (h + 1) * tok], top)
            low = jnp.where(lanes == h, denom[h * tok : (h + 1) * tok], low)
        numers.append(top)
        denoms.append(low)
    return jnp.concatenate(numers, axis=1), jnp.concatenate(denoms, axis=1)


def begin_body(query, pair, numer, denom):
    for r in range(0, query.shape[0], 256):
        rows = slice(r, min(r + 256, query.shape[0]))
        numer[rows], denom[rows] = absorb(query[rows], [pair])


def finish_body(first, query, numer, denom, inner, outer, out_weight, out):
    rows = slice(first, first + out.shape[0])
    top, low = absorb(query[rows], [inner, outer])
    context = ((numer[rows] + top) / (denom[rows] + low)).astype(BF16)
    out[...] = dot(context, out_weight[...]).astype(out.dtype)


def own_body(normed, weight, pair, inner, outer, out_weight, merged, out):
    top, low = absorb(query_of(normed[...], weight), [pair, inner, outer])
    out[...] = merged[...] + dot((top / low).astype(BF16), out_weight[...])


def shards(pixels, embed_weight, variable_embed, agg_key, agg_value, position, qkv_weight, out_weight):
    n = lax.axis_size("var")
    n_vars, n_pix, band_tok = pixels.shape
    d = embed_weight.shape[2]
    tok = position.shape[0]
    width = qkv_weight.shape[2]
    n_heads = agg_key.shape[1]
    all_vars = n_vars * n
    rows = n_vars * n_pix
    depth = rows * band_tok // d
    sds = jax.ShapeDtypeStruct
    table = embed_weight.reshape(rows, d)
    pix = pixels.reshape(rows, band_tok)
    key_t = jnp.transpose(agg_key)
    weight = jnp.transpose(qkv_weight, (1, 0, 2))

    shared, placed = call(
        pack_body,
        [sds((size, d), BF16) for size in (depth + rows // 2 + n_vars, depth + tok)],
        (table, variable_embed, pix, position),
        "pack",
        [pltpu.HBM] * 4,
        [pltpu.VMEM((n_vars, d), BF16), pltpu.SemaphoreType.DMA((3 + 2 * (d // band_tok),))],
    )
    others = range(1, n)
    near = [shifted(shared, "var", r) for r in others]
    outer = outward(placed)
    positions = [shifted(position, "var", r) for r in others]

    moved = (table, variable_embed, key_t, agg_value, weight, out_weight)
    key_t, agg_value, weight, out_weight, *folded = call(
        functools.partial(stage_body, len(moved)),
        [sds(a.shape, a.dtype) for a in moved[2:]]
        + [sds((d, rows), BF16), sds((n_vars * n_heads, d), BF16), sds((n_heads, rows), F32), sds((n_heads, n_vars), F32)],
        moved,
        "stage",
        [pltpu.HBM] * len(moved),
        [pltpu.VMEM((rows, d), BF16), pltpu.VMEM((n_vars, d), BF16), pltpu.SemaphoreType.DMA((len(moved),))],
    )
    near, _ = lax.optimization_barrier((near, folded[2]))
    packs = [shared] + near
    far = [inward(x[depth : depth + rows // 2]) for x in near]
    outer, _ = lax.optimization_barrier((outer, folded[0]))
    positions, _ = lax.optimization_barrier((positions, folded[1]))
    lead = 16
    cut = depth + lead
    outer_heads = [outer[:cut]] + [shifted(outer[:cut], "var", r) for r in others]
    outer_tails = [outer[cut:]] + [outward(x[lead:]) for x in positions]
    *folded, merged, normed, query, pair = call(
        functools.partial(band_body, n, depth),
        [
            sds((d, rows * n), BF16),
            sds((all_vars * n_heads, d), BF16),
            sds((n_heads, rows * n), F32),
            sds((n_heads, all_vars), F32),
            sds((tok, d), F32),
            sds((tok, d), BF16),
            sds((band_tok - tok, width), BF16),
            sds((2, band_tok, width), BF16),
        ],
        (*packs, *far, *folded, placed, *positions, key_t, agg_value, weight),
        "front_band",
        scratch=[pltpu.VMEM((rows, d), BF16)],
    )
    inner = inward(pair)
    totals = call(begin_body, [sds((band_tok - tok, width), F32)] * 2, (query, pair), "attend_band")
    *outer_heads, _ = lax.optimization_barrier((*outer_heads, totals[0]))
    (mixed,) = call(
        functools.partial(outer_mix_body, n, depth), [sds((band_tok, d), F32)], (*outer_heads, *folded), "mix_outer"
    )
    (ready,) = call(gate_body, [sds((8, 128), F32)], (mixed, *outer_tails[1:]), "gate")
    spans = [(0, tok * 5 // 8), (tok * 5 // 8, tok)]
    outer_pair, *share = call(
        functools.partial(outer_body, n, depth),
        [sds((2, band_tok, width), BF16)] + [sds((spans[0][1], d), BF16)] * (n > 1),
        (*outer_heads, *outer_tails, mixed, weight, query, *totals, inner, out_weight, ready),
        "front_outer",
    )
    attended = (query, *totals, inner, outer_pair, out_weight)
    pieces = [[None] * len(spans) for _ in others]
    for r in others:
        for i, (start, stop) in enumerate(spans):
            if r > 1 or i > 0:
                share = call(
                    functools.partial(finish_body, (r - 1) * tok + start), [sds((stop - start, d), BF16)], attended, "attend_later"
                )
            pieces[r - 1][i] = shifted(share[0], "var", n - r)
    (update,) = call(
        own_body, [sds((tok, d), F32)], (normed, weight, pair, inner, outer_pair, out_weight, merged), "attend_own"
    )
    for parts in pieces:
        update = update + jnp.concatenate(parts, axis=0).astype(F32)
    return update.astype(BF16)


def solution(mesh):
    in_specs = (
        P("var", None, "band"),
        P("var", None, None),
        P("var", None),
        P(),
        P(),
        P(("band", "var"), None),
        P(None, None, "var"),
        P("var", None),
    )
    out_specs = P(("band", "var"), None)
    return jax.shard_map(shards, mesh=mesh, in_specs=in_specs, out_specs=out_specs, check_vma=False)
```
